128 devices in a mesh: member: 8 (over z, y_lo), band: 16 (over x, y_hi, core).
Axes of the slice: x: 4, y: 4 (y_hi: 2, y_lo: 2; y = y_hi * 2 + y_lo), z: 4, core: 2. Of those that a mesh axis runs over, the one named last changes fastest.
Arguments:
- hidden: bfloat16 [16, 1024, 1024], P('member', 'band'), may hold values from -6 to 6
- queries: bfloat16 [4096, 1024], P('band'), may hold values from -6 to 6
- kv_weight: bfloat16 [1024, 2048], replicated, may hold values from -0.1875 to 0.1875
- out_weight: bfloat16 [1024, 1024], replicated, may hold values from -0.1875 to 0.1875
- head_projection: bfloat16 [1024, 100], replicated, may hold values from -0.1875 to 0.1875
- initial_state: float32 [100, 4096], P(None, 'band'), may hold values from -6 to 6
- truth: float32 [100, 4096], P(None, 'band'), may hold values from -8 to 8
- latitude_weight: float32 [4096], P('band'), may hold values from 0.1 to 2
- channel_loss_weight: float32 [100], replicated, may hold values from 0.3 to 3
- sources: int32 [3, 4096], P(None, 'band'), may hold values from 0 to 127, as said below
- halo_rows: int32 [32, 32], P('band'), may hold values from 0 to 63, as said below
Outputs:
- hidden_grad: float32 [16, 1024, 1024], P('member', 'band')
- kv_grad: float32 [1024, 2048], P(('member', 'band'))
- out_grad: float32 [1024, 1024], P(('member', 'band'))
- head_grad: float32 [1024, 100], P(('member', 'band'))
The draws below stay inside these ranges and needn't reach their ends.
Inputs may be any that keep to these rules, and one draw needn't show every extreme that they name: sources[e, t] names a row of the extended list of point t's band: rows below 64 are the band's own nodes, the next 32 those received from the band below, the last 32 those from the band above; the 3 rows of one point are distinct; the first band names no row from below and the last band none from above. `halo_rows`: rows 2 b and 2 b + 1 list the nodes of band b sent to the band below and to the band above; each node of a band stands once in the two rows together.
All inputs are finite; a program needn't handle non-finite values.
Results may differ from the reference program's by a relative error of at most 0.019.
Values may be sent and summed in bfloat16 or wider, within the bound.
A program may use at most 128 MiB of HBM per device.

```python
import math
import jax
import jax.numpy as jnp
from jax import lax

C = 1024
HEAD_DIM = 64
HEADS = 16
CH = 100
EDGES = 3
MEMBERS = 16
G_DEV = 256
HN_DEV = 64
HALO = 32
NGRID = 4096
HNODES = 1024
N_BAND = 16
DEVICES = 128


def shuffled_half(band_key):
    return jax.random.permutation(band_key, HN_DEV // 2).astype(jnp.int32)


def draw_latitude_weight(key, part):
    key = jax.random.fold_in(key, 5)
    point_count = G_DEV * N_BAND
    position = (jnp.arange(point_count, dtype=jnp.float32) + 0.5) / point_count
    smooth = 0.35 + 0.65 * jnp.sin(jnp.pi * position)
    rough_part = jax.random.uniform(key, (point_count,), jnp.float32, 0.6, 1.4)
    return smooth * rough_part


def draw_sources(key, part):
    key = jax.random.fold_in(key, 11)
    point_count = G_DEV * N_BAND
    point_index = jnp.arange(point_count, dtype=jnp.int32)
    band_index = point_index // G_DEV
    local_index = point_index % G_DEV
    base_node = local_index * (HN_DEV - 5 * EDGES) // G_DEV
    jitter = jax.random.randint(key, (EDGES, point_count), 0, 5, dtype=jnp.int32)
    jitter = jnp.where(local_index[None, :] == 0, 0, jitter)
    offsets = jnp.arange(EDGES, dtype=jnp.int32)[:, None] * 5
    nearby = base_node[None, :] + offsets + jitter
    halo_pick = jax.random.randint(jax.random.fold_in(key, 1), (point_count,), 0, HALO, dtype=jnp.int32)
    rim_points = G_DEV // 8
    halo_pick = jnp.where(local_index == rim_points - 1, HALO - 1, halo_pick)
    halo_pick = jnp.where(local_index == G_DEV - rim_points, HALO - 1, halo_pick)
    lower_rim = (local_index < rim_points) & (band_index > 0)
    upper_rim = (local_index >= G_DEV - rim_points) & (band_index < N_BAND - 1)
    first_edge = jnp.where(lower_rim, HN_DEV + halo_pick, jnp.where(upper_rim, HN_DEV + HALO + halo_pick, nearby[0]))
    return jnp.concatenate([first_edge[None, :], nearby[1:]], axis=0).astype(jnp.int32)


def draw_halo_rows(key, part):
    key = jax.random.fold_in(key, 23)
    band_keys = jax.random.split(key, 2 * N_BAND)
    picked = jax.vmap(shuffled_half)(band_keys)
    offsets = jnp.arange(2 * N_BAND, dtype=jnp.int32) % 2 * (HN_DEV // 2)
    return (picked + offsets[:, None]).astype(jnp.int32)


def with_spikes(result, key, source, target, parts, factor):
    def block_of(dim):
        return (jnp.arange(result.shape[dim]) // (result.shape[dim] // parts)).reshape((-1,) + (1,) * (result.ndim - 1 - dim))

    first = jax.random.permutation(key, parts)[block_of(target)]
    second = (block_of(target) + parts // 2) % parts
    return jnp.where((block_of(source) == first) | (block_of(source) == second), factor * result, result)


def steps_of(key, shape, pieces, low, top_value):
    factor_of = 1.0
    for dim, parts in pieces:
        draws = jax.random.uniform(jax.random.fold_in(jax.random.fold_in(key, 6), dim), (parts,), jnp.float32, low / len(pieces), top_value / len(pieces))
        factor_of = factor_of * jnp.repeat(jnp.exp(draws), shape[dim] // parts).reshape((-1,) + (1,) * (len(shape) - 1 - dim))
    return factor_of


def gaussian(rng, shape, deviation, bound, cuts=(), held_as=jnp.bfloat16):
    values = deviation * jax.random.normal(rng, shape, jnp.float32)
    if cuts:
        values = values * steps_of(rng, shape, cuts, -0.22, 0.18)
    return jnp.clip(values, -bound, bound).astype(held_as)


def heavy_noise(stream_key, shape, scale, bound, shards, heavy, kind=jnp.bfloat16):
    result = scale * jax.random.normal(stream_key, shape, jnp.float32)
    if shards:
        result = result * steps_of(stream_key, shape, shards, -0.22, 0.18)
    return jnp.clip(with_spikes(result, jax.random.fold_in(stream_key, 3), *heavy), -bound, bound).astype(kind)


def setup_inputs(seed: int = 0) -> dict:
    splits = jax.random.split(jax.random.key(seed), 12)
    hidden = heavy_noise(splits[0], (MEMBERS, HNODES, C), 1.0, 6.0, ((0, 8), (1, 16)), (1, 2, 16, 2.0))
    queries = gaussian(splits[1], (NGRID, C), 1.0, 6.0, ((0, 16),))
    kv_weight = gaussian(splits[2], (C, 2 * C), C ** -0.5, 0.1875)
    out_weight = gaussian(splits[3], (C, C), C ** -0.5, 0.1875)
    head_projection = gaussian(splits[4], (C, CH), C ** -0.5, 0.1875)
    initial_state = gaussian(splits[5], (CH, NGRID), 1.0, 6.0, ((1, 16),), jnp.float32)
    truth = gaussian(splits[6], (CH, NGRID), 1.5, 8.0, ((1, 16),), jnp.float32)
    latitude_weight = draw_latitude_weight(jax.random.fold_in(splits[11], 71), 0)
    channel_loss_weight = jnp.clip(jnp.exp(jax.random.uniform(splits[8], (CH,), jnp.float32, math.log(0.3), math.log(3.0))), 0.3, 3.0)
    sources = draw_sources(jax.random.fold_in(splits[11], 71), 0)
    halo_rows = draw_halo_rows(jax.random.fold_in(splits[11], 71), 0)
    return {"hidden": hidden, "queries": queries, "kv_weight": kv_weight, "out_weight": out_weight, "head_projection": head_projection, "initial_state": initial_state, "truth": truth, "latitude_weight": latitude_weight, "channel_loss_weight": channel_loss_weight, "sources": sources, "halo_rows": halo_rows}


ALPHA = 0.95
SOFTENING = 0.5

def pick_rows(node_rows, index_list):
    return node_rows[index_list]

def add_back(local_rows, index_list, lower_rows, upper_rows):
    return local_rows.at[index_list[0]].add(lower_rows).at[index_list[1]].add(upper_rows)

def reference(hidden, queries, kv_weight, out_weight, head_projection, initial_state, truth, latitude_weight, channel_loss_weight, sources, halo_rows):
    band_of_point = (jnp.arange(NGRID, dtype=jnp.int32) // G_DEV).astype(jnp.int32)
    node_ids = (sources + band_of_point[None, :] * (2 * HN_DEV)).astype(jnp.int32)
    index_lists = halo_rows.reshape(N_BAND, 2, HALO)
    query_heads = queries.reshape(NGRID, HEADS, HEAD_DIM)
    score_scale = HEAD_DIM ** (-0.5)

    def extend_nodes(ensemble_rows):
        band_rows = ensemble_rows.reshape(N_BAND, HN_DEV, C)
        picked = jax.vmap(pick_rows)(band_rows, index_lists)
        zero_block = jnp.zeros((1, HALO, C), jnp.bfloat16)
        from_below = jnp.concatenate([zero_block, picked[:-1, 1]], axis=0)
        from_above = jnp.concatenate([picked[1:, 0], zero_block], axis=0)
        return jnp.concatenate([band_rows, from_below, from_above], axis=1).reshape(N_BAND * 2 * HN_DEV, C)

    def member_forward_pass(ensemble_rows):
        extended_nodes = extend_nodes(ensemble_rows)
        key_value = jnp.dot(extended_nodes, kv_weight, preferred_element_type=jnp.float32).astype(jnp.bfloat16)
        key_value = lax.optimization_barrier(key_value)
        edge_rows = key_value[node_ids]
        edge_keys = edge_rows[..., :C].reshape(EDGES, NGRID, HEADS, HEAD_DIM)
        edge_messages = edge_rows[..., C:].reshape(EDGES, NGRID, HEADS, HEAD_DIM)
        scores = jnp.einsum('kthd,thd->kth', edge_keys.astype(jnp.float32), query_heads.astype(jnp.float32)) * score_scale
        gate_activations = jax.nn.sigmoid(scores)
        gate_lowprecision = lax.optimization_barrier(gate_activations.astype(jnp.bfloat16))
        combined_nodes = jnp.einsum('kth,kthd->thd', gate_lowprecision.astype(jnp.float32), edge_messages.astype(jnp.float32))
        combined_nodes = combined_nodes.reshape(NGRID, C).astype(jnp.bfloat16)
        updated = queries.astype(jnp.float32) + jnp.dot(combined_nodes, out_weight, preferred_element_type=jnp.float32)
        updated_lowprecision = updated.astype(jnp.bfloat16)
        prediction = initial_state + lax.dot_general(head_projection, updated_lowprecision, (((0,), (1,)), ((), ())), preferred_element_type=jnp.float32)
        return (extended_nodes, edge_messages, gate_activations, gate_lowprecision, combined_nodes, updated_lowprecision, prediction)

    def produce_prediction(ensemble_rows):
        return member_forward_pass(ensemble_rows)[-1]
    predictions = lax.map(produce_prediction, hidden)
    score_weight = channel_loss_weight[:, None] * latitude_weight[None, :]
    spread = (1.0 - (1.0 - ALPHA) / MEMBERS) / (MEMBERS * (MEMBERS - 1))

    def pairwise_terms(local_rows):
        member_differences = local_rows[None] - predictions
        gap_root = jnp.sqrt(member_differences * member_differences + SOFTENING * SOFTENING)
        slope_sum = lax.optimization_barrier(jnp.sum(member_differences / gap_root, axis=0))
        truth_gap = local_rows - truth
        truth_root = jnp.sqrt(truth_gap * truth_gap + SOFTENING * SOFTENING)
        return score_weight * (truth_gap / truth_root / MEMBERS - spread * slope_sum)
    loss_gradient_list = lax.map(pairwise_terms, predictions)
    grad_rounded = loss_gradient_list.astype(jnp.bfloat16)

    def member_step(running, inputs):
        ensemble_rows, member_grad = inputs
        kv_sum, out_sum, head_sum = running
        extended_nodes, edge_messages, gate_activations, gate_lowprecision, combined_nodes, updated_lowprecision, prediction = member_forward_pass(ensemble_rows)
        head_part = lax.dot_general(updated_lowprecision, member_grad, (((0,), (1,)), ((), ())), preferred_element_type=jnp.float32)
        update_grad = lax.dot_general(member_grad, head_projection, (((0,), (1,)), ((), ())), preferred_element_type=jnp.float32).astype(jnp.bfloat16)
        out_part = lax.dot_general(combined_nodes, update_grad, (((0,), (0,)), ((), ())), preferred_element_type=jnp.float32)
        merged_grad = lax.dot_general(update_grad, out_weight, (((1,), (1,)), ((), ())), preferred_element_type=jnp.float32).astype(jnp.bfloat16)
        merged_grad = lax.optimization_barrier(merged_grad).reshape(NGRID, HEADS, HEAD_DIM)
        gate_grad = jnp.einsum('thd,kthd->kth', merged_grad.astype(jnp.float32), edge_messages.astype(jnp.float32))
        score_grad = gate_grad * gate_activations * (1.0 - gate_activations) * score_scale
        value_grad = gate_lowprecision.astype(jnp.float32)[..., None] * merged_grad.astype(jnp.float32)[None]
        key_grad = score_grad[..., None] * query_heads.astype(jnp.float32)[None]
        edge_grad = jnp.concatenate([key_grad.reshape(EDGES, NGRID, C), value_grad.reshape(EDGES, NGRID, C)], axis=-1)
        node_grad = jax.ops.segment_sum(edge_grad.reshape(EDGES * NGRID, 2 * C), node_ids.reshape(-1), num_segments=N_BAND * 2 * HN_DEV)
        node_grad = node_grad.astype(jnp.bfloat16)
        kv_part = lax.dot_general(extended_nodes, node_grad, (((0,), (0,)), ((), ())), preferred_element_type=jnp.float32)
        extended_grad = lax.dot_general(node_grad, kv_weight, (((1,), (1,)), ((), ())), preferred_element_type=jnp.float32)
        band_grad = extended_grad.reshape(N_BAND, 2 * HN_DEV, C)
        own_grad = band_grad[:, :HN_DEV]
        below_grad = band_grad[:, HN_DEV:HN_DEV + HALO]
        above_grad = band_grad[:, HN_DEV + HALO:]
        zero_block = jnp.zeros((1, HALO, C), jnp.float32)
        to_upper_list = jnp.concatenate([below_grad[1:], zero_block], axis=0)
        to_lower_list = jnp.concatenate([zero_block, above_grad[:-1]], axis=0)
        hidden_part = jax.vmap(add_back)(own_grad, index_lists, to_lower_list, to_upper_list).reshape(HNODES, C)
        return ((kv_sum + kv_part, out_sum + out_part, head_sum + head_part), hidden_part)
    start_sums = (jnp.zeros((C, 2 * C), jnp.float32), jnp.zeros((C, C), jnp.float32), jnp.zeros((C, CH), jnp.float32))
    totals, hidden_grad = lax.scan(member_step, start_sums, (hidden, grad_rounded))
    kv_grad = totals[0] / DEVICES
    out_grad = totals[1] / DEVICES
    head_grad = totals[2] / DEVICES
    return (hidden_grad, kv_grad, out_grad, head_grad)
```

```python
import jax
import jax.numpy as jnp
from jax import lax
from jax.experimental import pallas as pl
from jax.experimental.pallas import tpu as pltpu
from jax.sharding import PartitionSpec as P

MESH = pl.DeviceIdType.MESH
BF = jnp.bfloat16
F32 = jnp.float32
ALPHA = 0.95
SOFTENING = 0.5
MEMBERS = 16
DEVICES = 128
NN = (((1,), (0,)), ((), ()))
NT = (((1,), (1,)), ((), ()))


def mm(a, b, dims=NN):
    return lax.dot_general(a, b, dims, preferred_element_type=F32)


def body(
    hid_hbm, q_hbm, kvw_hbm, ow_hbm, head, init, truth, lat, cw, src, halo,
    hg_out, kv_out, og_out, hd_out,
    ext, q3, kvw, ow, owt, qt, headp, headt, hgt, pick, lrow, kv3, mask, gt, dsg, um,
    initp, truthp, wts, f3, fg, lloc, l4, ug, dm, ah, ahr, nown, nsend, nrecv, nsnd, nrcv, nt,
    kvp, kvr, fsnd, frcv,
    in_sem, halo_s, halo_r, hid_s, hid_r, fc_s, fc_r, lg_s, lg_r, ah_s, ah_r, nh_s, nh_r,
    na_s, na_r, rs_s, rs_r, fin_s, fin_r,
):
    mem, band = lax.axis_index("member"), lax.axis_index("band")
    z, ylo = mem // 2, mem % 2
    core = band % 2
    group = z * 2 + core
    plane = ylo * 8 + band // 2

    def group_peer(j):
        return (j // 2) * 2 + ylo, band - core + j % 2

    def plane_peer(q):
        return z * 2 + q // 8, (q % 8) * 2 + core

    def member_peer(m):
        return m, band

    below, above = (mem, (band + 15) % 16), (mem, (band + 1) % 16)

    def each(count, fn):
        def step(k, carry):
            fn(k)
            return carry
        lax.fori_loop(1, count, step, 0)

    def remote(source, target, send, recv, device):
        return pltpu.make_async_remote_copy(
            src_ref=source, dst_ref=target, send_sem=send, recv_sem=recv,
            device_id=device, device_id_type=MESH)

    loads = [pltpu.make_async_copy(hid_hbm, ext.at[:, 0:2], in_sem.at[0]),
             pltpu.make_async_copy(kvw_hbm, kvw, in_sem.at[1]),
             pltpu.make_async_copy(ow_hbm, ow, in_sem.at[2])]
    loads += [pltpu.make_async_copy(q_hbm.at[:, 128 * p:128 * p + 128], q3.at[p], in_sem.at[3 + p])
              for p in range(8)]
    for copy in loads:
        copy.start()

    barrier = pltpu.get_barrier_semaphore()

    def greet(device):
        pl.semaphore_signal(barrier, inc=1, device_id=device, device_id_type=MESH)

    greet(below)
    greet(above)
    each(8, lambda k: greet(group_peer((group + k) % 8)))
    each(8, lambda k: greet(member_peer((mem + k) % 8)))
    each(16, lambda k: greet(plane_peer((plane + k) % 16)))

    for m in range(2):
        for d in range(2):
            at = 64 * m + 32 * d
            lrow[0:1, at:at + 32] = halo[d:d + 1, :] + 64 * m
    row_of = lax.broadcasted_iota(jnp.int32, (128, 128), 0)
    lane_of = lax.broadcasted_iota(jnp.int32, (128, 128), 1)
    scatter = (row_of == lrow[0:1, :]).astype(F32)
    gather = scatter.T.astype(BF)
    scatter = scatter.astype(BF)

    loads[0].wait()
    own = ext[:, 0:2].reshape(128, 1024)
    for n in range(4):
        cols = slice(256 * n, 256 * n + 256)
        pick[:, :, :, cols] = mm(gather, own[:, cols]).astype(BF).reshape(2, 2, 32, 256)

    pl.semaphore_wait(barrier, 31)
    to_below = remote(pick.at[:, 0], ext.at[:, 3], halo_s.at[0], halo_r.at[0], below)
    to_above = remote(pick.at[:, 1], ext.at[:, 2], halo_s.at[1], halo_r.at[1], above)
    to_below.start()
    to_above.start()

    mine = pl.ds(pl.multiple_of(group * 128, 128), 128)
    for n in range(8):
        rows = slice(128 * n, 128 * n + 128)
        hgt[rows, mine] = own[:, rows].T

    def hid_copy(k):
        return remote(hgt.at[:, mine], hgt.at[:, mine], hid_s.at[k], hid_r.at[k],
                      group_peer((group + k) % 8))

    each(8, lambda k: hid_copy(k).start())

    headp[...] = jnp.zeros_like(headp)
    headp[:, 0:100] = head[...]
    headt[...] = headp[...].T
    initp[...] = jnp.zeros_like(initp)
    initp[0:100, :] = init[...]
    truthp[...] = jnp.zeros_like(truthp)
    truthp[0:100, :] = truth[...]
    lrow[1:2, :] = jnp.zeros_like(lrow[1:2, :])
    diag = jnp.where(row_of == lane_of, cw[...], 0.0)
    wts[...] = jnp.sum(diag, axis=1, keepdims=True) * lat[...]
    point_row = lax.broadcasted_iota(jnp.int32, (128, 256), 0)
    edge = (point_row == src[0:1, :]) | (point_row == src[1:2, :]) | (point_row == src[2:3, :])
    mask[0:128, :] = edge.astype(F32)
    mask[128:256, :] = edge.astype(F32)
    lo_lane = (lane_of < 64).astype(BF)
    hi_lane = (lane_of >= 64).astype(BF)
    lo_row = (row_of < 64).astype(BF)
    hi_row = (row_of >= 64).astype(BF)
    for p in range(8):
        loads[3 + p].wait()
        qt[128 * p:128 * p + 128, :] = q3[p].T
    loads[2].wait()
    for i in range(4):
        rows = slice(256 * i, 256 * i + 256)
        for j in range(4):
            cols = slice(256 * j, 256 * j + 256)
            owt[rows, cols] = ow[cols, rows].T

    loads[1].wait()
    to_below.wait_recv()
    to_above.wait_recv()
    rows256 = ext[...].reshape(256, 1024)
    for n in range(8):
        part = mm(rows256, kvw[:, 256 * n:256 * n + 256]).astype(BF)
        kv3[2 * n] = part[:, :128]
        kv3[2 * n + 1] = part[:, 128:]

    def forward(p, carry):
        for m in range(2):
            kp = kv3[p, 128 * m:128 * m + 128, :]
            vt = kv3[8 + p, 128 * m:128 * m + 128, :].T
            kcat = jnp.concatenate([kp * lo_lane, kp * hi_lane], axis=0)
            score = mm(kcat, q3[p], NT)
            th = jnp.tanh(score * (0.5 / 8.0))
            on = mask[...]
            gate = ((0.5 + 0.5 * th) * on).astype(BF)
            gt[m, p] = gate
            dsg[m, p] = (0.25 - 0.25 * th * th) * (on * 0.125)
            vcat_t = jnp.concatenate([vt * lo_row, vt * hi_row], axis=1)
            um[m, pl.ds(pl.multiple_of(p * 128, 128), 128), :] = mm(vcat_t, gate).astype(BF)
        return carry

    lax.fori_loop(0, 8, forward, 0)

    for m in range(2):
        merged = um[m, 0:1024, :]
        for i in range(4):
            rows = slice(256 * i, 256 * i + 256)
            up = mm(owt[rows, :], merged) + qt[rows, :].astype(F32)
            um[m, 1024 + 256 * i:1024 + 256 * i + 256, :] = up.astype(BF)
        f3[m] = mm(headt[...], um[m, 1024:2048, :]) + initp[...]

    def fc_copy(k):
        to = (mem + k) % 8
        return remote(f3.at[:, pl.ds(pl.multiple_of(to * 16, 16), 16), :], fg.at[pl.ds(2 * mem, 2)],
                      fc_s.at[k], fc_r.at[k], member_peer(to))

    each(8, lambda k: fc_copy(k).start())
    my_rows = pl.ds(pl.multiple_of(mem * 16, 16), 16)
    for m in range(2):
        fg[2 * mem + m] = f3[m, my_rows, :]
    each(8, lambda k: remote(f3.at[:, my_rows, :], fg.at[pl.ds(2 * ((mem + 8 - k) % 8), 2)],
                             fc_s.at[k], fc_r.at[k], member_peer((mem + k) % 8)).wait_recv())

    spread = (1.0 - (1.0 - ALPHA) / MEMBERS) / (MEMBERS * (MEMBERS - 1))
    soft = SOFTENING * SOFTENING
    truth_rows = truthp[my_rows, :]
    weight = wts[my_rows, :]

    def loss(m, carry):
        f = fg[m]
        gap = f[None] - fg[...]
        slopes = jnp.sum(gap * lax.rsqrt(gap * gap + soft), axis=0)
        off = f - truth_rows
        slope = off * lax.rsqrt(off * off + soft)
        lloc[m] = (weight * (slope * (1.0 / MEMBERS) - spread * slopes)).astype(BF)
        return carry

    lax.fori_loop(0, MEMBERS, loss, 0)

    def lg_copy(k):
        to = (mem + k) % 8
        return remote(lloc.at[pl.ds(2 * to, 2)], l4.at[:, mem], lg_s.at[k], lg_r.at[k],
                      member_peer(to))

    each(8, lambda k: lg_copy(k).start())
    for m in range(2):
        l4[m, mem] = lloc[2 * mem + m]
    each(8, lambda k: remote(lloc.at[pl.ds(2 * mem, 2)], l4.at[:, (mem + 8 - k) % 8],
                             lg_s.at[k], lg_r.at[k], member_peer((mem + k) % 8)).wait_recv())

    for m in range(2):
        grad = l4[m].reshape(128, 256)
        for i in range(4):
            rows = slice(256 * i, 256 * i + 256)
            ug[m, rows, :] = mm(headp[rows, :], grad).astype(BF)
        for i in range(4):
            rows = slice(256 * i, 256 * i + 256)
            dm[m, rows, :] = mm(ow[rows, :], ug[m]).astype(BF)

    low = lane_of < 64

    def backward(p, carry):
        for m in range(2):
            vp = kv3[8 + p, 128 * m:128 * m + 128, :]
            vcat = jnp.concatenate([vp * lo_lane, vp * hi_lane], axis=0)
            grad = dm[m, pl.ds(pl.multiple_of(p * 128, 128), 128), :]
            score_grad = (mm(vcat, grad) * dsg[m, p]).astype(BF)
            dk = mm(score_grad, q3[p])
            dv = mm(gt[m, p], grad, NT)
            for c, both in ((p, dk), (8 + p, dv)):
                rows = jnp.where(low, both[:128], both[128:])
                nown[c, 64 * m:64 * m + 64, :] = rows[0:64]
                nsend[0, c, m] = rows[64:96].astype(BF)
                nsend[1, c, m] = rows[96:128].astype(BF)
        return carry

    lax.fori_loop(0, 8, backward, 0)
    back_below = remote(nsend.at[0], nrecv.at[:, :, 1], nh_s.at[0], nh_r.at[0], below)
    back_above = remote(nsend.at[1], nrecv.at[:, :, 0], nh_s.at[1], nh_r.at[1], above)
    back_below.start()
    back_above.start()

    for a in range(2):
        for i in range(4):
            rows = slice(1024 * a + 256 * i, 1024 * a + 256 * i + 256)
            both = mm(um[0, rows, :], l4[0].reshape(128, 256), NT) + mm(
                um[1, rows, :], l4[1].reshape(128, 256), NT)
            ah[a, i] = both.astype(BF).reshape(16, 16, 128)

    def ah_copy(k):
        to = (plane + k) % 16
        return remote(ah.at[:, :, to], ahr.at[plane], ah_s.at[k], ah_r.at[k], plane_peer(to))

    each(16, lambda k: ah_copy(k).start())
    ahr[plane] = ah[:, :, plane]

    back_below.wait_recv()
    back_above.wait_recv()
    for c in range(16):
        total = nown[c] + mm(scatter, nrecv[c].reshape(128, 128))
        rounded = total.astype(BF)
        nt[:, 128 * c:128 * c + 128] = rounded
        nsnd[c // 2, :, 128 * (c % 2):128 * (c % 2) + 128] = rounded

    def na_copy(k):
        to = (group + k) % 8
        return remote(nsnd.at[to], nrcv.at[group], na_s.at[k], na_r.at[k], group_peer(to))

    each(8, lambda k: na_copy(k).start())
    nrcv[group] = nsnd[group]

    for i in range(4):
        rows = slice(256 * i, 256 * i + 256)
        hg_out[:, rows] = mm(nt[...], kvw[rows, :], NT)

    each(8, lambda k: remote(hgt.at[:, mine], hgt.at[:, pl.ds(pl.multiple_of(((group + 8 - k) % 8) * 128, 128), 128)],
                             hid_s.at[k], hid_r.at[k], group_peer((group + k) % 8)).wait_recv())
    each(8, lambda k: remote(nsnd.at[group], nrcv.at[(group + 8 - k) % 8], na_s.at[k], na_r.at[k],
                             group_peer((group + k) % 8)).wait_recv())
    cols256 = nrcv[...].reshape(1024, 256)
    for i in range(4):
        rows = slice(256 * i, 256 * i + 256)
        kvp[i] = mm(hgt[rows, :], cols256).astype(BF).reshape(16, 16, 256)

    def rs_copy(k):
        to = (plane + k) % 16
        return remote(kvp.at[:, to], kvr.at[plane], rs_s.at[k], rs_r.at[k], plane_peer(to))

    each(16, lambda k: rs_copy(k).start())
    kvr[plane] = kvp[:, plane]

    each(16, lambda k: remote(ah.at[:, :, plane], ahr.at[(plane + 16 - k) % 16], ah_s.at[k], ah_r.at[k],
                              plane_peer((plane + k) % 16)).wait_recv())
    ah_sum = jnp.sum(ahr[...].astype(F32), axis=0)
    fsnd[:, 8:16, 0:128] = ah_sum[0].reshape(8, 8, 128)
    fsnd[:, 8:16, 128:256] = ah_sum[1].reshape(8, 8, 128)
    each(16, lambda k: remote(kvp.at[:, plane], kvr.at[(plane + 16 - k) % 16], rs_s.at[k], rs_r.at[k],
                              plane_peer((plane + k) % 16)).wait_recv())
    fsnd[:, 0:8, :] = jnp.sum(kvr[...].astype(F32), axis=0).reshape(8, 8, 256)

    def fin_copy(k):
        to = (group + k) % 8
        return remote(fsnd.at[to], frcv.at[group], fin_s.at[k], fin_r.at[k], group_peer(to))

    each(8, lambda k: fin_copy(k).start())
    frcv[group] = fsnd[group]
    each(8, lambda k: remote(fsnd.at[group], frcv.at[(group + 8 - k) % 8], fin_s.at[k], fin_r.at[k],
                             group_peer((group + k) % 8)).wait_recv())
    for j in range(8):
        kv_out[:, 256 * j:256 * j + 256] = frcv[j, 0:8, :] * (1.0 / DEVICES)
    sums = jnp.sum(frcv[:, 8:16, :], axis=0) * (1.0 / DEVICES)
    hd_out[...] = sums[:, 128:228]
    outer = sums[:, 0:128]
    big = outer.astype(BF)
    small = (outer - big.astype(F32)).astype(BF)
    og_out[...] = mm(big, headt[...]) + mm(small, headt[...])

    to_below.wait_send()
    to_above.wait_send()
    back_below.wait_send()
    back_above.wait_send()
    for count, copy in ((8, hid_copy), (8, fc_copy), (8, lg_copy), (8, na_copy), (8, fin_copy),
                        (16, ah_copy), (16, rs_copy)):
        each(count, lambda k, copy=copy: copy(k).wait_send())


def shards(hidden, queries, kv_weight, out_weight, head_projection, initial_state, truth,
           latitude_weight, channel_loss_weight, sources, halo_rows):
    vmem = pl.BlockSpec(memory_space=pltpu.VMEM)
    hbm = pl.BlockSpec(memory_space=pl.ANY)
    dma = pltpu.SemaphoreType.DMA
    scratch = [
        ((2, 4, 32, 1024), BF), ((8, 256, 128), BF), ((1024, 2048), BF), ((1024, 1024), BF),
        ((1024, 1024), BF), ((1024, 256), BF), ((1024, 128), BF), ((128, 1024), BF),
        ((1024, 1024), BF), ((2, 2, 32, 1024), BF), ((8, 128), jnp.int32), ((16, 256, 128), BF),
        ((256, 256), F32), ((2, 8, 256, 256), BF), ((2, 8, 256, 256), F32), ((2, 2048, 256), BF),
        ((128, 256), F32), ((128, 256), F32), ((128, 256), F32), ((2, 128, 256), F32),
        ((16, 16, 256), F32), ((16, 16, 256), BF), ((2, 8, 16, 256), BF), ((2, 1024, 256), BF),
        ((2, 1024, 256), BF), ((2, 4, 16, 16, 128), BF), ((16, 2, 4, 16, 128), BF),
        ((16, 128, 128), F32), ((2, 16, 2, 32, 128), BF), ((16, 2, 2, 32, 128), BF),
        ((8, 128, 256), BF), ((8, 128, 256), BF), ((128, 2048), BF), ((4, 16, 16, 256), BF),
        ((16, 4, 16, 256), BF), ((8, 16, 256), F32), ((8, 16, 256), F32),
    ]
    sems = [11, 2, 2, 8, 8, 8, 8, 8, 8, 16, 16, 2, 2, 8, 8, 16, 16, 8, 8]
    hidden_grad, kv_grad, out_grad, head_grad = pl.pallas_call(
        body,
        out_shape=[jax.ShapeDtypeStruct((128, 1024), F32), jax.ShapeDtypeStruct((8, 2048), F32),
                   jax.ShapeDtypeStruct((8, 1024), F32), jax.ShapeDtypeStruct((8, 100), F32)],
        in_specs=[hbm] * 4 + [vmem] * 7,
        out_specs=[vmem] * 4,
        scratch_shapes=[pltpu.VMEM(shape, kind) for shape, kind in scratch] + [dma((n,)) for n in sems],
        compiler_params=pltpu.CompilerParams(
            collective_id=0, has_side_effects=True, vmem_limit_bytes=56 * 1024 * 1024),
    )(
        hidden.reshape(2, 2, 32, 1024), queries, kv_weight, out_weight, head_projection,
        initial_state, truth, latitude_weight.reshape(1, 256),
        jnp.pad(channel_loss_weight, (0, 28)).reshape(1, 128), sources, halo_rows,
    )
    return hidden_grad.reshape(2, 64, 1024), kv_grad, out_grad, head_grad


def solution(mesh):
    placed = (
        P("member", "band", None),
        P("band", None),
        P(),
        P(),
        P(),
        P(None, "band"),
        P(None, "band"),
        P("band"),
        P(),
        P(None, "band"),
        P("band", None),
    )
    return jax.shard_map(
        shards,
        mesh=mesh,
        in_specs=placed,
        out_specs=(
            P("member", "band", None),
            P(("member", "band"), None),
            P(("member", "band"), None),
            P(("member", "band"), None),
        ),
        check_vma=False,
    )
```

```python
import jax
import jax.numpy as jnp
from jax import lax
from jax.experimental import pallas as pl
from jax.experimental.pallas import tpu as pltpu
from jax.sharding import PartitionSpec as P

MESH = pl.DeviceIdType.MESH
BF = jnp.bfloat16
F32 = jnp.float32
ALPHA = 0.95
SOFTENING = 0.5
MEMBERS = 16
DEVICES = 128
NN = (((1,), (0,)), ((), ()))
NT = (((1,), (1,)), ((), ()))


def mm(a, b, dims=NN):
    return lax.dot_general(a, b, dims, preferred_element_type=F32)


def body(
    hid_hbm, q_hbm, kvw_hbm, ow_hbm, head, init, truth, lat, cw, src, halo,
    hg_hbm, frcv, headt,
    ext, q3, kvw, ow, owt, qt, headp, hgt, pick, lrow, kv3, mask, gt, dsg, um,
    initp, truthp, wts, f3, fg, lloc, l4, ug, dm, ah, ahx, ahs, ahr, nown, nsend, nrecv, nsnd, nrcv, nt,
    kvp, kvr, fsnd, hg,
    in_sem, out_sem, halo_s, halo_r, hid_s, hid_r, sib_s, sib_r, fc_s, fc_r, lg_s, lg_r, ah_s, ah_r, nh_s, nh_r,
    na_s, na_r, rs_s, rs_r, fin_s, fin_r, ax_s, ax_r,
):
    mem, band = lax.axis_index("member"), lax.axis_index("band")
    z, ylo = mem // 2, mem % 2
    core = band % 2
    group = z * 2 + core
    plane = ylo * 8 + band // 2

    def group_peer(j):
        return (j // 2) * 2 + ylo, band - core + j % 2

    def plane_peer(q):
        return z * 2 + q // 8, (q % 8) * 2 + core

    def member_peer(m):
        return m, band

    pending = []

    sib_group = group + 1 - 2 * core
    sibling = (mem, band + 1 - 2 * core)
    below, above = (mem, (band + 15) % 16), (mem, (band + 1) % 16)

    def each(count, fn):
        def step(k, carry):
            fn(k)
            return carry
        lax.fori_loop(1, count, step, 0)

    def remote(source, target, send, recv, device):
        return pltpu.make_async_remote_copy(
            src_ref=source, dst_ref=target, send_sem=send, recv_sem=recv,
            device_id=device, device_id_type=MESH)

    loads = [pltpu.make_async_copy(hid_hbm, ext.at[:, 0:2], in_sem.at[0]),
             pltpu.make_async_copy(kvw_hbm, kvw, in_sem.at[1]),
             pltpu.make_async_copy(ow_hbm, ow, in_sem.at[2])]
    loads += [pltpu.make_async_copy(q_hbm.at[:, 128 * p:128 * p + 128], q3.at[p], in_sem.at[3 + p])
              for p in range(8)]
    for copy in loads:
        copy.start()

    barrier = pltpu.get_barrier_semaphore()

    def greet(device):
        pl.semaphore_signal(barrier, inc=1, device_id=device, device_id_type=MESH)

    greet(below)
    greet(above)
    each(8, lambda k: greet(group_peer((group + k) % 8)))
    for k in range(4):
        greet(member_peer((mem + 2 * k + 1) % 8))
    each(16, lambda k: greet(plane_peer((plane + k) % 16)))

    for m in range(2):
        for d in range(2):
            at = 64 * m + 32 * d
            lrow[0:1, at:at + 32] = halo[d:d + 1, :] + 64 * m
    row_of = lax.broadcasted_iota(jnp.int32, (128, 128), 0)
    lane_of = lax.broadcasted_iota(jnp.int32, (128, 128), 1)
    scatter = (row_of == lrow[0:1, :]).astype(F32)
    gather = scatter.T.astype(BF)
    scatter = scatter.astype(BF)

    loads[0].wait()
    own = ext[:, 0:2].reshape(128, 1024)
    for n in range(4):
        cols = slice(256 * n, 256 * n + 256)
        pick[:, :, :, cols] = mm(gather, own[:, cols]).astype(BF).reshape(2, 2, 32, 256)

    pl.semaphore_wait(barrier, 28)
    to_below = remote(pick.at[:, 0], ext.at[:, 3], halo_s.at[0], halo_r.at[0], below)
    to_above = remote(pick.at[:, 1], ext.at[:, 2], halo_s.at[1], halo_r.at[1], above)
    to_below.start()
    to_above.start()
    pending.append((1, lambda k: to_below))
    pending.append((1, lambda k: to_above))

    mine = pl.ds(pl.multiple_of(group * 128, 128), 128)
    for n in range(8):
        rows = slice(128 * n, 128 * n + 128)
        hgt[rows, mine] = own[:, rows].T

    def hid_columns(j):
        return hgt.at[:, pl.ds(pl.multiple_of(j * 128, 128), 128)]

    def hid_copy(k):
        return remote(hid_columns(group), hid_columns(group), hid_s.at[k], hid_r.at[k],
                      group_peer((group + 2 * k) % 8))

    def hid_wait(k):
        return remote(hid_columns(group), hid_columns((group + 8 - 2 * k) % 8), hid_s.at[k],
                      hid_r.at[k], group_peer((group + 2 * k) % 8))

    def sib_copy(k):
        block = hid_columns((group + 8 - 2 * k) % 8)
        return remote(block, block, sib_s.at[k], sib_r.at[k], sibling)

    def sib_wait(k):
        block = hid_columns((sib_group + 8 - 2 * k) % 8)
        return remote(block, block, sib_s.at[k], sib_r.at[k], sibling)

    each(4, lambda k: hid_copy(k).start())
    pending.append((4, hid_copy))
    sib_copy(0).start()
    pending.append((1, sib_copy))

    headt[...] = jnp.zeros_like(headt)
    headt[0:100, :] = head[...]
    headp[...] = headt[...].T
    initp[...] = jnp.zeros_like(initp)
    initp[0:100, :] = init[...]
    truthp[...] = jnp.zeros_like(truthp)
    truthp[0:100, :] = truth[...]
    wts[...] = jnp.zeros_like(wts)
    wts[0:1, 0:100] = cw[...]
    diag = jnp.where(row_of == lane_of, wts[0:1, 0:128], 0.0)
    wts[...] = jnp.sum(diag, axis=1, keepdims=True) * lat[...]
    point_row = lax.broadcasted_iota(jnp.int32, (128, 256), 0)
    edge = (point_row == src[0:1, :]) | (point_row == src[1:2, :]) | (point_row == src[2:3, :])
    mask[0:128, :] = edge.astype(F32)
    mask[128:256, :] = edge.astype(F32)
    lo_lane = (lane_of < 64).astype(BF)
    hi_lane = (lane_of >= 64).astype(BF)
    lo_row = (row_of < 64).astype(BF)
    hi_row = (row_of >= 64).astype(BF)
    for p in range(8):
        loads[3 + p].wait()
        qt[128 * p:128 * p + 128, :] = q3[p].T
    loads[2].wait()
    for i in range(4):
        rows = slice(256 * i, 256 * i + 256)
        for j in range(4):
            cols = slice(256 * j, 256 * j + 256)
            owt[rows, cols] = ow[cols, rows].T

    loads[1].wait()
    to_below.wait_recv()
    to_above.wait_recv()
    rows256 = ext[...].reshape(256, 1024)
    for n in range(8):
        part = mm(rows256, kvw[:, 256 * n:256 * n + 256]).astype(BF)
        kv3[2 * n] = part[:, :128]
        kv3[2 * n + 1] = part[:, 128:]

    def forward(p, carry):
        for m in range(2):
            kp = kv3[p, 128 * m:128 * m + 128, :]
            vt = kv3[8 + p, 128 * m:128 * m + 128, :].T
            kcat = jnp.concatenate([kp * lo_lane, kp * hi_lane], axis=0)
            score = mm(kcat, q3[p], NT)
            th = jnp.tanh(score * (0.5 / 8.0))
            on = mask[...]
            gate = ((0.5 + 0.5 * th) * on).astype(BF)
            gt[m, p] = gate
            dsg[m, p] = (0.25 - 0.25 * th * th) * (on * 0.125)
            vcat_t = jnp.concatenate([vt * lo_row, vt * hi_row], axis=1)
            um[m, pl.ds(pl.multiple_of(p * 128, 128), 128), :] = mm(vcat_t, gate).astype(BF)
        return carry

    lax.fori_loop(0, 8, forward, 0)

    each(4, lambda k: hid_wait(k).wait_recv())
    each(4, lambda k: sib_copy(k).start())
    pending.append((4, sib_copy))

    for m in range(2):
        merged = um[m, 0:1024, :]
        for i in range(4):
            rows = slice(256 * i, 256 * i + 256)
            up = mm(owt[rows, :], merged) + qt[rows, :].astype(F32)
            um[m, 1024 + 256 * i:1024 + 256 * i + 256, :] = up.astype(BF)
        f3[m] = mm(headt[...], um[m, 1024:2048, :]) + initp[...]

    def fc_copy(k):
        to = (mem + k) % 8
        return remote(f3.at[:, pl.ds(pl.multiple_of(to * 16, 16), 16), :], fg.at[pl.ds(2 * mem, 2)],
                      fc_s.at[k], fc_r.at[k], member_peer(to))

    each(8, lambda k: fc_copy(k).start())
    pending.append((8, fc_copy))
    my_rows = pl.ds(pl.multiple_of(mem * 16, 16), 16)
    for m in range(2):
        fg[2 * mem + m] = f3[m, my_rows, :]
    each(8, lambda k: remote(f3.at[:, my_rows, :], fg.at[pl.ds(2 * ((mem + 8 - k) % 8), 2)],
                             fc_s.at[k], fc_r.at[k], member_peer((mem + k) % 8)).wait_recv())

    spread = (1.0 - (1.0 - ALPHA) / MEMBERS) / (MEMBERS * (MEMBERS - 1))
    soft = SOFTENING * SOFTENING
    truth_rows = truthp[my_rows, :]
    weight = wts[my_rows, :]

    def loss(m, carry):
        f = fg[m]
        gap = f[None] - fg[...]
        slopes = jnp.sum(gap * lax.rsqrt(gap * gap + soft), axis=0)
        off = f - truth_rows
        slope = off * lax.rsqrt(off * off + soft)
        lloc[m] = (weight * (slope * (1.0 / MEMBERS) - spread * slopes)).astype(BF)
        return carry

    lax.fori_loop(0, MEMBERS, loss, 0)

    def lg_copy(k):
        to = (mem + k) % 8
        return remote(lloc.at[pl.ds(2 * to, 2)], l4.at[:, mem], lg_s.at[k], lg_r.at[k],
                      member_peer(to))

    each(8, lambda k: lg_copy(k).start())
    pending.append((8, lg_copy))
    for m in range(2):
        l4[m, mem] = lloc[2 * mem + m]
    each(8, lambda k: remote(lloc.at[pl.ds(2 * mem, 2)], l4.at[:, (mem + 8 - k) % 8],
                             lg_s.at[k], lg_r.at[k], member_peer((mem + k) % 8)).wait_recv())

    for m in range(2):
        grad = l4[m].reshape(128, 256)
        for i in range(4):
            rows = slice(256 * i, 256 * i + 256)
            ug[m, rows, :] = mm(headp[rows, :], grad).astype(BF)
        for i in range(4):
            rows = slice(256 * i, 256 * i + 256)
            dm[m, rows, :] = mm(ow[rows, :], ug[m]).astype(BF)

    low = lane_of < 64

    def backward(p, carry):
        for m in range(2):
            vp = kv3[8 + p, 128 * m:128 * m + 128, :]
            vcat = jnp.concatenate([vp * lo_lane, vp * hi_lane], axis=0)
            grad = dm[m, pl.ds(pl.multiple_of(p * 128, 128), 128), :]
            score_grad = (mm(vcat, grad) * dsg[m, p]).astype(BF)
            dk = mm(score_grad, q3[p])
            dv = mm(gt[m, p], grad, NT)
            for c, both in ((p, dk), (8 + p, dv)):
                rows = jnp.where(low, both[:128], both[128:])
                nown[c, 64 * m:64 * m + 64, :] = rows[0:64]
                nsend[0, c, m] = rows[64:96].astype(BF)
                nsend[1, c, m] = rows[96:128].astype(BF)
        return carry

    lax.fori_loop(0, 8, backward, 0)
    back_below = remote(nsend.at[0], nrecv.at[:, :, 1], nh_s.at[0], nh_r.at[0], below)
    back_above = remote(nsend.at[1], nrecv.at[:, :, 0], nh_s.at[1], nh_r.at[1], above)
    back_below.start()
    back_above.start()
    pending.append((1, lambda k: back_below))
    pending.append((1, lambda k: back_above))

    for a in range(2):
        for i in range(4):
            rows = slice(1024 * a + 256 * i, 1024 * a + 256 * i + 256)
            both = mm(um[0, rows, :], l4[0].reshape(128, 256), NT) + mm(
                um[1, rows, :], l4[1].reshape(128, 256), NT)
            ah[i % 2, a, i // 2] = both.astype(BF)
    swap = remote(ah.at[1 - core], ahx, ax_s.at[0], ax_r.at[0], sibling)
    swap.start()
    pending.append((1, lambda k: swap))

    back_below.wait_recv()
    back_above.wait_recv()
    for c in range(16):
        total = nown[c] + mm(scatter, nrecv[c].reshape(128, 128))
        rounded = total.astype(BF)
        nt[:, 128 * c:128 * c + 128] = rounded
        nsnd[c // 2, :, 128 * (c % 2):128 * (c % 2) + 128] = rounded

    def na_copy(k):
        to = (group + k) % 8
        return remote(nsnd.at[to], nrcv.at[group], na_s.at[k], na_r.at[k], group_peer(to))

    each(8, lambda k: na_copy(k).start())
    pending.append((8, na_copy))
    nrcv[group] = nsnd[group]

    swap.wait_recv()
    for a in range(2):
        for i in range(2):
            both = ah[core, a, i].astype(F32) + ahx[a, i].astype(F32)
            ahs[a, i] = both.astype(BF).reshape(16, 16, 128)

    def ah_copy(k):
        to = (plane + k) % 16
        return remote(ahs.at[:, :, to], ahr.at[plane], ah_s.at[k], ah_r.at[k], plane_peer(to))

    each(16, lambda k: ah_copy(k).start())
    pending.append((16, ah_copy))
    ahr[plane] = ahs[:, :, plane]

    for i in range(4):
        rows = slice(256 * i, 256 * i + 256)
        hg[:, rows] = mm(nt[...], kvw[rows, :], NT)
    hg_copy = pltpu.make_async_copy(hg, hg_hbm, out_sem.at[0])
    hg_copy.start()

    sib_wait(0).wait_recv()
    each(4, lambda k: sib_wait(k).wait_recv())
    each(8, lambda k: remote(nsnd.at[group], nrcv.at[(group + 8 - k) % 8], na_s.at[k], na_r.at[k],
                             group_peer((group + k) % 8)).wait_recv())
    cols256 = nrcv[...].reshape(1024, 256)
    for i in range(4):
        rows = slice(256 * i, 256 * i + 256)
        kvp[i] = mm(hgt[rows, :], cols256).astype(BF).reshape(16, 16, 256)

    def rs_copy(k):
        to = (plane + k) % 16
        return remote(kvp.at[:, to], kvr.at[plane], rs_s.at[k], rs_r.at[k], plane_peer(to))

    each(16, lambda k: rs_copy(k).start())
    pending.append((16, rs_copy))
    kvr[plane] = kvp[:, plane]

    each(16, lambda k: remote(ahs.at[:, :, plane], ahr.at[(plane + 16 - k) % 16], ah_s.at[k], ah_r.at[k],
                              plane_peer((plane + k) % 16)).wait_recv())
    ah_sum = jnp.sum(ahr[...].astype(F32), axis=0)
    for i in range(2):
        for c in range(2):
            at = (2 * i + core) * 2 + c
            fsnd[at, 8:16, 0:128] = ah_sum[0, i, 8 * c:8 * c + 8]
            fsnd[at, 8:16, 128:256] = ah_sum[1, i, 8 * c:8 * c + 8]
            other = (2 * i + 1 - core) * 2 + c
            fsnd[other, 8:16, :] = jnp.zeros((8, 256), F32)
    each(16, lambda k: remote(kvp.at[:, plane], kvr.at[(plane + 16 - k) % 16], rs_s.at[k], rs_r.at[k],
                              plane_peer((plane + k) % 16)).wait_recv())
    fsnd[:, 0:8, :] = jnp.sum(kvr[...].astype(F32), axis=0).reshape(8, 8, 256)

    def fin_copy(k):
        to = (group + k) % 8
        return remote(fsnd.at[to], frcv.at[group], fin_s.at[k], fin_r.at[k], group_peer(to))

    each(8, lambda k: fin_copy(k).start())
    pending.append((8, fin_copy))
    frcv[group] = fsnd[group]
    each(8, lambda k: remote(fsnd.at[group], frcv.at[(group + 8 - k) % 8], fin_s.at[k], fin_r.at[k],
                             group_peer((group + k) % 8)).wait_recv())
    hg_copy.wait()

    for count, copy in pending:
        if count == 1:
            copy(0).wait_send()
        else:
            each(count, lambda k, copy=copy: copy(k).wait_send())


def finish(hg, frcv, headt, hg_out, kv_out, og_out, hd_out, sem):
    copy = pltpu.make_async_copy(hg, hg_out, sem)
    copy.start()
    for j in range(8):
        kv_out[:, 256 * j:256 * j + 256] = frcv[j, 0:8, :] * (1.0 / DEVICES)
    sums = jnp.sum(frcv[:, 8:16, :], axis=0) * (1.0 / DEVICES)
    hd_out[...] = sums[:, 128:228]
    outer = sums[:, 0:128]
    big = outer.astype(BF)
    small = (outer - big.astype(F32)).astype(BF)
    og_out[...] = mm(big, headt[...]) + mm(small, headt[...])
    copy.wait()


def shards(hidden, queries, kv_weight, out_weight, head_projection, initial_state, truth,
           latitude_weight, channel_loss_weight, sources, halo_rows):
    vmem = pl.BlockSpec(memory_space=pltpu.VMEM)
    hbm = pl.BlockSpec(memory_space=pl.ANY)
    dma = pltpu.SemaphoreType.DMA
    scratch = [
        ((2, 4, 32, 1024), BF), ((8, 256, 128), BF), ((1024, 2048), BF), ((1024, 1024), BF),
        ((1024, 1024), BF), ((1024, 256), BF), ((1024, 128), BF),
        ((1024, 1024), BF), ((2, 2, 32, 1024), BF), ((8, 128), jnp.int32), ((16, 256, 128), BF),
        ((256, 256), F32), ((2, 8, 256, 256), BF), ((2, 8, 256, 256), F32), ((2, 2048, 256), BF),
        ((128, 256), F32), ((128, 256), F32), ((128, 256), F32), ((2, 128, 256), F32),
        ((16, 16, 256), F32), ((16, 16, 256), BF), ((2, 8, 16, 256), BF), ((2, 1024, 256), BF),
        ((2, 1024, 256), BF), ((2, 2, 2, 256, 128), BF), ((2, 2, 256, 128), BF),
        ((2, 2, 16, 16, 128), BF), ((16, 2, 2, 16, 128), BF),
        ((16, 128, 128), F32), ((2, 16, 2, 32, 128), BF), ((16, 2, 2, 32, 128), BF),
        ((8, 128, 256), BF), ((8, 128, 256), BF), ((128, 2048), BF), ((4, 16, 16, 256), BF),
        ((16, 4, 16, 256), BF), ((8, 16, 256), F32), ((128, 1024), F32),
    ]
    sems = [11, 1, 2, 2, 4, 4, 4, 4, 8, 8, 8, 8, 16, 16, 2, 2, 8, 8, 16, 16, 8, 8, 1, 1]
    raw_hidden, raw_sums, head_rows = pl.pallas_call(
        body,
        out_shape=[jax.ShapeDtypeStruct((128, 1024), F32), jax.ShapeDtypeStruct((8, 16, 256), F32),
                   jax.ShapeDtypeStruct((128, 1024), BF)],
        in_specs=[hbm] * 4 + [vmem] * 7,
        out_specs=[hbm, vmem, vmem],
        scratch_shapes=[pltpu.VMEM(shape, kind) for shape, kind in scratch] + [dma((n,)) for n in sems],
        compiler_params=pltpu.CompilerParams(
            collective_id=0, has_side_effects=True, vmem_limit_bytes=56 * 1024 * 1024),
    )(
        hidden.reshape(2, 2, 32, 1024), queries, kv_weight, out_weight, head_projection.T,
        initial_state, truth, latitude_weight.reshape(1, 256), channel_loss_weight.reshape(1, 100),
        sources, halo_rows,
    )
    hidden_grad, kv_grad, out_grad, head_grad = pl.pallas_call(
        finish,
        out_shape=[jax.ShapeDtypeStruct((128, 1024), F32), jax.ShapeDtypeStruct((8, 2048), F32),
                   jax.ShapeDtypeStruct((8, 1024), F32), jax.ShapeDtypeStruct((8, 100), F32)],
        in_specs=[vmem, vmem, vmem],
        out_specs=[hbm, vmem, vmem, vmem],
        scratch_shapes=[dma(())],
    )(raw_hidden, raw_sums, head_rows)
    return hidden_grad.reshape(2, 64, 1024), kv_grad, out_grad, head_grad


def solution(mesh):
    placed = (
        P("member", "band", None),
        P("band", None),
        P(),
        P(),
        P(),
        P(None, "band"),
        P(None, "band"),
        P("band"),
        P(),
        P(None, "band"),
        P("band", None),
    )
    return jax.shard_map(
        shards,
        mesh=mesh,
        in_specs=placed,
        out_specs=(
            P("member", "band", None),
            P(("member", "band"), None),
            P(("member", "band"), None),
            P(("member", "band"), None),
        ),
        check_vma=False,
    )
```

```python
import jax
import jax.numpy as jnp
from jax import lax
from jax.experimental import pallas as pl
from jax.experimental.pallas import tpu as pltpu
from jax.sharding import PartitionSpec as P

MESH = pl.DeviceIdType.MESH
BF = jnp.bfloat16
F32 = jnp.float32
ALPHA = 0.95
SOFTENING = 0.5
MEMBERS = 16
DEVICES = 128
NN = (((1,), (0,)), ((), ()))
NT = (((1,), (1,)), ((), ()))


def mm(a, b, dims=NN):
    return lax.dot_general(a, b, dims, preferred_element_type=F32)


def rem(a, n):
    return lax.rem(a, jnp.int32(n))


def div(a, n):
    return lax.div(a, jnp.int32(n))


def body(
    hid_hbm, q_hbm, kvw_hbm, ow_hbm, head, init, truth, lat, cw, src, halo,
    hg_hbm, frcv,
    ext, q3, kvw, ow, owt, qt, headp, headt, hgt, pick, lrow, kv3, mask, gt, dsg, um,
    initp, truthp, wts, f3, fg, lloc, l4, ug, dm, ah, ahx, ahs, ahr, nown, nsend, nrecv, nt, nsnd,
    nrcv, kvp, kvr, fsnd, hg,
    in_sem, out_sem, halo_s, halo_r, hid_s, hid_r, sib_s, sib_r, fc_s, fc_r, lg_s, lg_r,
    ah_s, ah_r, nh_s, nh_r, na_s, na_r, rs_s, rs_r, fin_s, fin_r, ax_s, ax_r,
):
    mem, band = lax.axis_index("member"), lax.axis_index("band")
    z, ylo = div(mem, 2), rem(mem, 2)
    core = rem(band, 2)
    group = z * 2 + core
    plane = ylo * 8 + div(band, 2)
    sibling = (mem, band + 1 - 2 * core)
    below, above = (mem, rem(band + 15, 16)), (mem, rem(band + 1, 16))
    pending = []

    def group_peer(j):
        return div(j, 2) * 2 + ylo, band - core + rem(j, 2)

    def plane_peer(q):
        return z * 2 + div(q, 8), rem(q, 8) * 2 + core

    def member_peer(m):
        return m, band

    def remote(source, target, send, recv, device):
        return pltpu.make_async_remote_copy(
            src_ref=source, dst_ref=target, send_sem=send, recv_sem=recv,
            device_id=device, device_id_type=MESH)

    def sent(bulk, send, recv):
        pending.append(remote(bulk, bulk, send, recv, sibling))

    def received(bulk, send, recv):
        remote(bulk, bulk, send, recv, sibling).wait_recv()

    def flush():
        while pending:
            pending.pop(0).wait_send()

    loads = [pltpu.make_async_copy(hid_hbm, ext.at[:, 0:2], in_sem.at[0]),
             pltpu.make_async_copy(kvw_hbm, kvw, in_sem.at[1]),
             pltpu.make_async_copy(ow_hbm, ow, in_sem.at[2])]
    loads += [pltpu.make_async_copy(q_hbm.at[:, 128 * p:128 * p + 128], q3.at[p], in_sem.at[3 + p])
              for p in range(8)]
    for copy in loads:
        copy.start()

    barrier = pltpu.get_barrier_semaphore()

    def greet(device):
        pl.semaphore_signal(barrier, inc=1, device_id=device, device_id_type=MESH)

    greet(below)
    greet(above)
    for k in range(1, 8):
        greet(group_peer(rem(group + k, 8)))
    for k in range(4):
        greet(member_peer(rem(mem + 2 * k + 1, 8)))
    for k in range(1, 16):
        greet(plane_peer(rem(plane + k, 16)))

    for m in range(2):
        for d in range(2):
            at = 64 * m + 32 * d
            lrow[0:1, at:at + 32] = halo[d:d + 1, :] + 64 * m
    row_of = lax.broadcasted_iota(jnp.int32, (128, 128), 0)
    lane_of = lax.broadcasted_iota(jnp.int32, (128, 128), 1)
    scatter = (row_of == lrow[0:1, :]).astype(F32)
    gather = scatter.T.astype(BF)
    scatter = scatter.astype(BF)

    loads[0].wait()
    own = ext[:, 0:2].reshape(128, 1024)
    for n in range(4):
        cols = slice(256 * n, 256 * n + 256)
        pick[:, :, :, cols] = mm(gather, own[:, cols]).astype(BF).reshape(2, 2, 32, 256)

    pl.semaphore_wait(barrier, 28)
    to_below = remote(pick.at[:, 0], ext.at[:, 3], halo_s.at[0], halo_r.at[0], below)
    to_above = remote(pick.at[:, 1], ext.at[:, 2], halo_s.at[1], halo_r.at[1], above)
    to_below.start()
    to_above.start()
    pending.extend([to_below, to_above])

    mine = pl.ds(pl.multiple_of(group * 128, 128), 128)
    for n in range(8):
        rows = slice(128 * n, 128 * n + 128)
        hgt[rows, mine] = own[:, rows].T

    def hid_columns(j):
        return hgt.at[:, pl.ds(pl.multiple_of(j * 128, 128), 128)]

    for k in (2, 1, 3):
        remote(hid_columns(group), hid_columns(group), hid_s, hid_r,
               group_peer(rem(group + 2 * k, 8))).start()
    remote(hid_columns(group), hid_columns(group), sib_s, sib_r, sibling).start()

    headt[...] = jnp.zeros_like(headt)
    headt[0:100, :] = head[...]
    headp[...] = headt[...].T
    initp[...] = jnp.zeros_like(initp)
    initp[0:100, :] = init[...]
    truthp[...] = jnp.zeros_like(truthp)
    truthp[0:100, :] = truth[...]
    wts[...] = jnp.zeros_like(wts)
    wts[0:1, 0:100] = cw[...]
    diag = jnp.where(row_of == lane_of, wts[0:1, 0:128], 0.0)
    wts[...] = jnp.sum(diag, axis=1, keepdims=True) * lat[...]
    point_row = lax.broadcasted_iota(jnp.int32, (128, 256), 0)
    edge = (point_row == src[0:1, :]) | (point_row == src[1:2, :]) | (point_row == src[2:3, :])
    mask[0:128, :] = edge.astype(F32)
    mask[128:256, :] = edge.astype(F32)
    lo_lane = (lane_of < 64).astype(BF)
    hi_lane = (lane_of >= 64).astype(BF)
    lo_row = (row_of < 64).astype(BF)
    hi_row = (row_of >= 64).astype(BF)
    for p in range(8):
        loads[3 + p].wait()
        qt[128 * p:128 * p + 128, :] = q3[p].T
    loads[2].wait()
    for i in range(4):
        rows = slice(256 * i, 256 * i + 256)
        for j in range(4):
            cols = slice(256 * j, 256 * j + 256)
            owt[rows, cols] = ow[cols, rows].T

    loads[1].wait()
    to_below.wait_recv()
    to_above.wait_recv()
    rows256 = ext[...].reshape(256, 1024)
    for n in range(8):
        part = mm(rows256, kvw[:, 256 * n:256 * n + 256]).astype(BF)
        kv3[2 * n] = part[:, :128]
        kv3[2 * n + 1] = part[:, 128:]

    my_rows = pl.ds(pl.multiple_of(mem * 16, 16), 16)
    for m in range(2):
        for p in range(8):
            kp = kv3[p, 128 * m:128 * m + 128, :]
            vt = kv3[8 + p, 128 * m:128 * m + 128, :].T
            kcat = jnp.concatenate([kp * lo_lane, kp * hi_lane], axis=0)
            score = mm(kcat, q3[p], NT)
            th = jnp.tanh(score * (0.5 / 8.0))
            on = mask[...]
            gate = ((0.5 + 0.5 * th) * on).astype(BF)
            gt[m, p] = gate
            dsg[m, p] = (0.25 - 0.25 * th * th) * (on * 0.125)
            vcat_t = jnp.concatenate([vt * lo_row, vt * hi_row], axis=1)
            um[m, 128 * p:128 * p + 128, :] = mm(vcat_t, gate).astype(BF)
        merged = um[m, 0:1024, :]
        for i in range(4):
            rows = slice(256 * i, 256 * i + 256)
            up = mm(owt[rows, :], merged) + qt[rows, :].astype(F32)
            um[m, 1024 + 256 * i:1024 + 256 * i + 256, :] = up.astype(BF)
        f3[m] = mm(headt[...], um[m, 1024:2048, :]) + initp[...]
        for k in range(7, 0, -1):
            to = rem(mem + k, 8)
            remote(f3.at[m, pl.ds(pl.multiple_of(to * 16, 16), 16), :], fg.at[2 * mem + m],
                   fc_s.at[m], fc_r.at[m], member_peer(to)).start()
        sent(fg.at[0:7], fc_s.at[m], fc_r.at[m])
        fg[2 * mem + m] = f3[m, my_rows, :]

    sent(hgt.at[:, 0:384], hid_s, hid_r)
    received(hgt.at[:, 0:384], hid_s, hid_r)
    for k in (1, 2, 3):
        block = hid_columns(rem(group + 2 * k, 8))
        remote(block, block, sib_s, sib_r, sibling).start()
    sent(hgt.at[:, 0:512], sib_s, sib_r)
    for m in range(2):
        received(fg.at[0:7], fc_s.at[m], fc_r.at[m])

    spread = (1.0 - (1.0 - ALPHA) / MEMBERS) / (MEMBERS * (MEMBERS - 1))
    soft = SOFTENING * SOFTENING
    truth_rows = truthp[my_rows, :]
    weight = wts[my_rows, :]

    for k in (4, 3, 5, 2, 6, 1, 7, 0):
        to = rem(mem + k, 8)
        for i in range(2):
            f = fg[2 * to + i]
            gap = f[None] - fg[...]
            slopes = jnp.sum(gap * lax.rsqrt(gap * gap + soft), axis=0)
            off = f - truth_rows
            slope = off * lax.rsqrt(off * off + soft)
            lloc[2 * to + i] = (weight * (slope * (1.0 / MEMBERS) - spread * slopes)).astype(BF)
        if k:
            remote(lloc.at[pl.ds(2 * to, 2)], l4.at[:, mem], lg_s, lg_r, member_peer(to)).start()
    sent(lloc.at[0:14], lg_s, lg_r)
    for m in range(2):
        l4[m, mem] = lloc[2 * mem + m]
    received(lloc.at[0:14], lg_s, lg_r)

    for m in range(2):
        grad = l4[m].reshape(128, 256)
        for i in range(4):
            rows = slice(256 * i, 256 * i + 256)
            ug[m, rows, :] = mm(headp[rows, :], grad).astype(BF)
    low = lane_of < 64
    order = (2, 1, 3, 0)

    def back_copy(h, step, d, inward=False):
        g = rem(z + order[step], 4)
        side = d if inward else 1 - d
        return remote(nsend.at[d, h, g], nrecv.at[h, g, :, side], nh_s.at[h, step, d],
                      nh_r.at[h, step, side], (below, above)[d])

    def keep(h, g, i, m, both):
        cols = slice(128 * i, 128 * i + 128)
        rows = jnp.where(low, both[:128], both[128:])
        nown[h, g, 64 * m:64 * m + 64, cols] = rows[0:64]
        nsend[0, h, g, m, :, cols] = rows[64:96].astype(BF)
        nsend[1, h, g, m, :, cols] = rows[96:128].astype(BF)

    def send_back(h, step):
        for d in range(2):
            copy = back_copy(h, step, d)
            copy.start()
            pending.append(copy)

    for step in range(4):
        g = rem(z + order[step], 4)
        rows = pl.ds(pl.multiple_of(g * 256, 256), 256)
        for m in range(2):
            dm[m, rows, :] = mm(ow[rows, :], ug[m]).astype(BF)
        for i in range(2):
            p = 2 * g + i
            for m in range(2):
                grad = dm[m, pl.ds(pl.multiple_of(p * 128, 128), 128), :]
                keep(0, g, i, m, mm(gt[m, p], grad, NT))
        send_back(0, step)
    for step in range(4):
        g = rem(z + order[step], 4)
        for i in range(2):
            p = 2 * g + i
            for m in range(2):
                vp = kv3[8 + p, 128 * m:128 * m + 128, :]
                vcat = jnp.concatenate([vp * lo_lane, vp * hi_lane], axis=0)
                grad = dm[m, pl.ds(pl.multiple_of(p * 128, 128), 128), :]
                score_grad = (mm(vcat, grad) * dsg[m, p]).astype(BF)
                keep(1, g, i, m, mm(score_grad, q3[p]))
        send_back(1, step)

    def node_step(h, step):
        g = rem(z + order[step], 4)
        for d in range(2):
            back_copy(h, step, d, True).wait_recv()
        total = (nown[h, g] + mm(scatter, nrecv[h, g].reshape(128, 256))).astype(BF)
        nt[:, pl.ds(pl.multiple_of(1024 * (1 - h) + g * 256, 256), 256)] = total
        for c in range(2):
            nsnd[h, 2 * g + c] = total[:, 128 * c:128 * c + 128]
        if step < 3:
            for c in range(2):
                remote(nsnd.at[h, 2 * g + c], nrcv.at[h, group], na_s.at[h], na_r.at[h],
                       group_peer(2 * g + c)).start()
        else:
            remote(nsnd.at[h, group + 1 - 2 * core], nrcv.at[h, group], na_s.at[h], na_r.at[h],
                   sibling).start()
            sent(nrcv.at[h, 0:7], na_s.at[h], na_r.at[h])
            nrcv[h, group] = nsnd[h, group]

    for step in range(4):
        node_step(0, step)

    for a in range(2):
        for i in range(4):
            rows = slice(1024 * a + 256 * i, 1024 * a + 256 * i + 256)
            both = mm(um[0, rows, :], l4[0].reshape(128, 256), NT) + mm(
                um[1, rows, :], l4[1].reshape(128, 256), NT)
            ah[i % 2, a, i // 2] = both.astype(BF)
    swap = remote(ah.at[1 - core], ahx, ax_s, ax_r, sibling)
    swap.start()
    pending.append(swap)

    for step in range(4):
        node_step(1, step)

    swap.wait_recv()
    for a in range(2):
        for i in range(2):
            both = ah[core, a, i].astype(F32) + ahx[a, i].astype(F32)
            ahs[a, i] = both.astype(BF).reshape(16, 16, 128)
    for k in range(1, 16):
        to = rem(plane + k, 16)
        remote(ahs.at[:, :, to], ahr.at[plane], ah_s, ah_r, plane_peer(to)).start()
    sent(ahr.at[0:15], ah_s, ah_r)
    ahr[plane] = ahs[:, :, plane]

    received(hgt.at[:, 0:512], sib_s, sib_r)
    for h in range(2):
        received(nrcv.at[h, 0:7], na_s.at[h], na_r.at[h])
        node_cols = nrcv[h].reshape(1024, 128)
        for i in range(4):
            rows = slice(256 * i, 256 * i + 256)
            kvp[h, i] = mm(hgt[rows, :], node_cols).astype(BF).reshape(16, 16, 128)
        for k in range(1, 16):
            to = rem(plane + k, 16)
            remote(kvp.at[h, :, to], kvr.at[h, plane], rs_s.at[h], rs_r.at[h], plane_peer(to)).start()
        kvr[h, plane] = kvp[h, :, plane]

    for i in range(4):
        rows = slice(256 * i, 256 * i + 256)
        hg[:, rows] = mm(nt[...], kvw[rows, :], NT)
    hg_copy = pltpu.make_async_copy(hg, hg_hbm, out_sem)
    hg_copy.start()
    flush()

    received(ahr.at[0:15], ah_s, ah_r)
    ah_sum = jnp.sum(ahr[...].astype(F32), axis=0)
    for i in range(2):
        for c in range(2):
            at = (2 * i + core) * 2 + c
            fsnd[at, 8:16, 0:128] = ah_sum[0, i, 8 * c:8 * c + 8]
            fsnd[at, 8:16, 128:256] = ah_sum[1, i, 8 * c:8 * c + 8]
            other = (2 * i + 1 - core) * 2 + c
            fsnd[other, 8:16, :] = jnp.zeros((8, 256), F32)
    for h in range(2):
        received(kvr.at[h, 0:15], rs_s.at[h], rs_r.at[h])
        kv_sum = jnp.sum(kvr[h].astype(F32), axis=0)
        fsnd[:, 0:8, 128 * h:128 * h + 128] = kv_sum.reshape(8, 8, 128)
    for k in (4, 5, 2, 3, 6, 7, 1):
        to = rem(group + k, 8)
        remote(fsnd.at[to], frcv.at[group], fin_s, fin_r, group_peer(to)).start()
    frcv[group] = fsnd[group]
    for h in range(2):
        sent(kvr.at[h, 0:15], rs_s.at[h], rs_r.at[h])
    sent(fsnd.at[0:7], fin_s, fin_r)
    flush()
    hg_copy.wait()
    received(frcv.at[0:7], fin_s, fin_r)


def finish(hg, frcv, head, hg_out, kv_out, og_out, hd_out, headt, sem):
    copy = pltpu.make_async_copy(hg, hg_out, sem)
    copy.start()
    headt[...] = jnp.zeros_like(headt)
    headt[0:100, :] = head[...]
    for j in range(8):
        at = 128 * j
        kv_out[:, at:at + 128] = frcv[j, 0:8, 128:256] * (1.0 / DEVICES)
        kv_out[:, 1024 + at:1024 + at + 128] = frcv[j, 0:8, 0:128] * (1.0 / DEVICES)
    sums = jnp.sum(frcv[:, 8:16, :], axis=0) * (1.0 / DEVICES)
    hd_out[...] = sums[:, 128:228]
    outer = sums[:, 0:128]
    big = outer.astype(BF)
    small = (outer - big.astype(F32)).astype(BF)
    og_out[...] = mm(big, headt[...]) + mm(small, headt[...])
    copy.wait()


def shards(hidden, queries, kv_weight, out_weight, head_projection, initial_state, truth,
           latitude_weight, channel_loss_weight, sources, halo_rows):
    vmem = pl.BlockSpec(memory_space=pltpu.VMEM)
    hbm = pl.BlockSpec(memory_space=pl.ANY)
    dma = pltpu.SemaphoreType.DMA
    scratch = [
        ((2, 4, 32, 1024), BF), ((8, 256, 128), BF), ((1024, 2048), BF), ((1024, 1024), BF),
        ((1024, 1024), BF), ((1024, 256), BF), ((1024, 128), BF), ((128, 1024), BF),
        ((1024, 1024), BF), ((2, 2, 32, 1024), BF), ((8, 128), jnp.int32), ((16, 256, 128), BF),
        ((256, 256), F32), ((2, 8, 256, 256), BF), ((2, 8, 256, 256), F32), ((2, 2048, 256), BF),
        ((128, 256), F32), ((128, 256), F32), ((128, 256), F32), ((2, 128, 256), F32),
        ((16, 16, 256), F32), ((16, 16, 256), BF), ((2, 8, 16, 256), BF), ((2, 1024, 256), BF),
        ((2, 1024, 256), BF), ((2, 2, 2, 256, 128), BF), ((2, 2, 256, 128), BF),
        ((2, 2, 16, 16, 128), BF), ((16, 2, 2, 16, 128), BF),
        ((2, 4, 128, 256), F32), ((2, 2, 4, 2, 32, 256), BF), ((2, 4, 2, 2, 32, 256), BF),
        ((128, 2048), BF), ((2, 8, 128, 128), BF), ((2, 8, 128, 128), BF),
        ((2, 4, 16, 16, 128), BF), ((2, 16, 4, 16, 128), BF), ((8, 16, 256), F32),
        ((128, 1024), F32),
    ]
    sems = [(11,), (), (2,), (2,), (), (), (), (), (2,), (2,), (), (), (), (), (2, 4, 2), (2, 4, 2),
            (2,), (2,), (2,), (2,), (), (), (), ()]
    raw_hidden, raw_sums = pl.pallas_call(
        body,
        out_shape=[jax.ShapeDtypeStruct((128, 1024), F32), jax.ShapeDtypeStruct((8, 16, 256), F32)],
        in_specs=[hbm] * 4 + [vmem] * 7,
        out_specs=[hbm, vmem],
        scratch_shapes=[pltpu.VMEM(shape, kind) for shape, kind in scratch] + [dma(n) for n in sems],
        compiler_params=pltpu.CompilerParams(
            collective_id=0, has_side_effects=True, vmem_limit_bytes=56 * 1024 * 1024),
    )(
        hidden.reshape(2, 2, 32, 1024), queries, kv_weight, out_weight, head_projection.T,
        initial_state, truth, latitude_weight.reshape(1, 256), channel_loss_weight.reshape(1, 100),
        sources, halo_rows,
    )
    hidden_grad, kv_grad, out_grad, head_grad = pl.pallas_call(
        finish,
        out_shape=[jax.ShapeDtypeStruct((128, 1024), F32), jax.ShapeDtypeStruct((8, 2048), F32),
                   jax.ShapeDtypeStruct((8, 1024), F32), jax.ShapeDtypeStruct((8, 100), F32)],
        in_specs=[vmem, vmem, vmem],
        out_specs=[hbm, vmem, vmem, vmem],
        scratch_shapes=[pltpu.VMEM((128, 1024), BF), dma(())],
    )(raw_hidden, raw_sums, head_projection.T)
    return hidden_grad.reshape(2, 64, 1024), kv_grad, out_grad, head_grad


def solution(mesh):
    placed = (
        P("member", "band", None),
        P("band", None),
        P(),
        P(),
        P(),
        P(None, "band"),
        P(None, "band"),
        P("band"),
        P(),
        P(None, "band"),
        P("band", None),
    )
    return jax.shard_map(
        shards,
        mesh=mesh,
        in_specs=placed,
        out_specs=(
            P("member", "band", None),
            P(("member", "band"), None),
            P(("member", "band"), None),
            P(("member", "band"), None),
        ),
        check_vma=False,
    )
```

```python
import jax
import jax.numpy as jnp
from jax import lax
from jax.experimental import pallas as pl
from jax.experimental.pallas import tpu as pltpu
from jax.sharding import PartitionSpec as P

MESH = pl.DeviceIdType.MESH
BF = jnp.bfloat16
F32 = jnp.float32
ALPHA = 0.95
SOFTENING = 0.5
MEMBERS = 16
DEVICES = 128
NN = (((1,), (0,)), ((), ()))
NT = (((1,), (1,)), ((), ()))


def mm(a, b, dims=NN):
    return lax.dot_general(a, b, dims, preferred_element_type=F32)


def rem(a, n):
    return lax.rem(a, jnp.int32(n))


def div(a, n):
    return lax.div(a, jnp.int32(n))


def body(
    hid_hbm, q_hbm, kvw_hbm, ow_hbm, head_hbm, init_hbm, truth_hbm, lat_hbm, cw_hbm, src_hbm, halo_hbm,
    hg_hbm, frcv,
    head, init, truth, lat, cw, src, halo,
    ext, q3, kvw, ow, owt, qt, headp, headt, hgt, pick, lrow, kvo, kvh, vto, mask, gt, dsg, um,
    initp, truthp, wts, f3, fg, lloc, l4, ug, dm, ah, ahx, ahs, ahr, ahs2, ahr2, nown, nsend, nrecv, nt, nsnd,
    nrcv, kvp, kvr, fsnd, hg,
    in_sem, out_sem, halo_s, halo_r, hid_s, hid_r, sib_s, sib_r, fc_s, fc_r, lg_s, lg_r,
    ah_s, ah_r, ay_s, ay_r, nh_s, nh_r, na_s, na_r, rs_s, rs_r, fin_s, fin_r, ax_s, ax_r,
):
    mem, band = lax.axis_index("member"), lax.axis_index("band")
    z, ylo = div(mem, 2), rem(mem, 2)
    core = rem(band, 2)
    group = z * 2 + core
    plane = ylo * 8 + div(band, 2)
    x, yhi = div(band, 4), rem(div(band, 2), 2)
    y = yhi * 2 + ylo
    sibling = (mem, band + 1 - 2 * core)
    below, above = (mem, rem(band + 15, 16)), (mem, rem(band + 1, 16))
    pending = []

    def group_peer(j):
        return div(j, 2) * 2 + ylo, band - core + rem(j, 2)

    def plane_peer(q):
        return z * 2 + div(q, 8), rem(q, 8) * 2 + core

    def member_peer(m):
        return m, band

    def remote(source, target, send, recv, device):
        return pltpu.make_async_remote_copy(
            src_ref=source, dst_ref=target, send_sem=send, recv_sem=recv,
            device_id=device, device_id_type=MESH)

    def sent(bulk, send, recv):
        pending.append(remote(bulk, bulk, send, recv, sibling))

    def received(bulk, send, recv):
        remote(bulk, bulk, send, recv, sibling).wait_recv()

    def flush():
        while pending:
            pending.pop(0).wait_send()

    loads = [pltpu.make_async_copy(source, target, in_sem.at[i]) for i, (source, target) in enumerate([
        (halo_hbm, halo), (hid_hbm, ext.at[:, 0:2]), (src_hbm, src), (lat_hbm, lat), (cw_hbm, cw),
        (init_hbm, init), (truth_hbm, truth), (head_hbm, head), (ow_hbm, ow), (kvw_hbm, kvw)])]
    loads += [pltpu.make_async_copy(q_hbm.at[:, 128 * p:128 * p + 128], q3.at[p], in_sem.at[10 + p])
              for p in range(8)]
    loads[0].start()
    loads[1].start()

    barrier = pltpu.get_barrier_semaphore()

    def greet(device):
        pl.semaphore_signal(barrier, inc=1, device_id=device, device_id_type=MESH)

    for k in (10, 9, 11, 6, 5, 7, 8, 2, 13, 14, 3, 1, 15, 4, 12):
        greet(plane_peer(rem(plane + k, 16)))
    greet(below)
    greet(above)
    for k in range(4):
        greet(member_peer(rem(mem + 2 * k + 1, 8)))
    for k in range(1, 8):
        greet(group_peer(rem(group + k, 8)))

    loads[0].wait()
    for m in range(2):
        for d in range(2):
            at = 64 * d + 32 * m
            lrow[0:1, at:at + 32] = halo[d:d + 1, :] + 64 * m
    row_of = lax.broadcasted_iota(jnp.int32, (128, 128), 0)
    lane_of = lax.broadcasted_iota(jnp.int32, (128, 128), 1)
    scatter = (row_of == lrow[0:1, :]).astype(F32)
    gather = scatter.T.astype(BF)
    scatter = scatter.astype(BF)

    loads[1].wait()
    for copy in loads[2:8] + loads[10:] + loads[8:10]:
        copy.start()
    own = ext[:, 0:2].reshape(128, 1024)
    for n in range(4):
        cols = slice(256 * n, 256 * n + 256)
        pick[:, :, :, cols] = mm(gather, own[:, cols]).astype(BF).reshape(2, 2, 32, 256)

    pl.semaphore_wait(barrier, 28)
    to_below = remote(pick.at[0], ext.at[:, 3], halo_s.at[0], halo_r.at[0], below)
    to_above = remote(pick.at[1], ext.at[:, 2], halo_s.at[1], halo_r.at[1], above)
    to_below.start()
    to_above.start()
    pending.extend([to_below, to_above])

    for n in range(8):
        rows = slice(128 * n, 128 * n + 128)
        hgt[group, rows, :] = own[:, rows].T
    pieces = (pl.ds(0, 512), pl.ds(512, 256), pl.ds(768, 256))

    def hid_piece(a, j):
        return hgt.at[j, pieces[a]]

    def hid_bulk(a):
        return hgt.at[0:3, pieces[a]]

    def hid_send(a):
        for k in (2, 1, 3):
            remote(hid_piece(a, group), hid_piece(a, group), hid_s.at[a], hid_r.at[a],
                   group_peer(rem(group + 2 * k, 8))).start()
        sent(hid_bulk(a), hid_s.at[a], hid_r.at[a])

    def hid_forward(a):
        received(hid_bulk(a), hid_s.at[a], hid_r.at[a])
        for k in (1, 2, 3):
            block = hid_piece(a, rem(group + 2 * k, 8))
            remote(block, block, sib_s.at[a], sib_r.at[a], sibling).start()
        sent(hid_bulk(a), sib_s.at[a], sib_r.at[a])

    hid_send(0)
    remote(hgt.at[group], hgt.at[group], sib_s.at[3], sib_r.at[3], sibling).start()
    sent(hgt.at[0], sib_s.at[3], sib_r.at[3])

    for copy in loads[2:8]:
        copy.wait()
    headt[...] = jnp.zeros_like(headt)
    headt[0:100, :] = head[...]
    headp[...] = headt[...].T
    initp[...] = jnp.zeros_like(initp)
    initp[0:100, :] = init[...]
    truthp[...] = jnp.zeros_like(truthp)
    truthp[0:100, :] = truth[...]
    wts[...] = jnp.zeros_like(wts)
    wts[0:1, 0:100] = cw[...]
    diag = jnp.where(row_of == lane_of, wts[0:1, 0:128], 0.0)
    wts[...] = jnp.sum(diag, axis=1, keepdims=True) * lat[...]
    point_row = lax.broadcasted_iota(jnp.int32, (128, 256), 0)
    edge = (point_row == src[0:1, :]) | (point_row == src[1:2, :]) | (point_row == src[2:3, :])
    edge = edge.astype(F32)
    for at in (0, 64):
        mask[at:at + 64, :] = edge[0:64]
        mask[128 + at:128 + at + 64, :] = edge[64:128]
    lo_lane = (lane_of < 64).astype(BF)[0:64]
    hi_lane = (lane_of >= 64).astype(BF)[0:64]
    for p in range(8):
        loads[10 + p].wait()
        qt[128 * p:128 * p + 128, :] = q3[p].T
    loads[8].wait()
    for i in range(4):
        rows = slice(256 * i, 256 * i + 256)
        for j in range(4):
            cols = slice(256 * j, 256 * j + 256)
            owt[rows, cols] = ow[cols, rows].T

    def project(rows, target):
        for n in range(8):
            part = mm(rows, kvw[:, 256 * n:256 * n + 256]).astype(BF)
            target[2 * n] = part[:, :128]
            target[2 * n + 1] = part[:, 128:]

    def by_head(block):
        return jnp.concatenate([block * lo_lane, block * hi_lane], axis=0)

    def gates(part, source, m, p):
        at = slice(128 * part, 128 * part + 128)
        score = mm(by_head(source[p, 64 * m:64 * m + 64, :]), q3[p], NT)
        th = jnp.tanh(score * (0.5 / 8.0))
        on = mask[at, :]
        gate = ((0.5 + 0.5 * th) * on).astype(BF)
        gt[m, p, at, :] = gate
        dsg[m, p, at, :] = (0.25 - 0.25 * th * th) * (on * 0.125)
        return gate

    loads[9].wait()
    project(own, kvo)
    for m in range(2):
        for p in range(8):
            gates(0, kvo, m, p)
            vto[m, p] = by_head(kvo[8 + p, 64 * m:64 * m + 64, :]).T
    to_below.wait_recv()
    to_above.wait_recv()
    project(ext[:, 2:4].reshape(128, 1024), kvh)

    my_rows = pl.ds(pl.multiple_of(mem * 16, 16), 16)
    for m in range(2):
        for p in range(8):
            gate = jnp.concatenate([gt[m, p, 0:128, :], gates(1, kvh, m, p)], axis=0)
            value = by_head(kvh[8 + p, 64 * m:64 * m + 64, :]).T
            value = jnp.concatenate([vto[m, p], value], axis=1)
            um[m, 128 * p:128 * p + 128, :] = mm(value, gate).astype(BF)
        merged = um[m, 0:1024, :]
        for i in range(4):
            rows = slice(256 * i, 256 * i + 256)
            up = mm(owt[rows, :], merged) + qt[rows, :].astype(F32)
            um[m, 1024 + 256 * i:1024 + 256 * i + 256, :] = up.astype(BF)
        f3[m] = mm(headt[...], um[m, 1024:2048, :]) + initp[...]
        for k in range(7, 0, -1):
            to = rem(mem + k, 8)
            remote(f3.at[m, pl.ds(pl.multiple_of(to * 16, 16), 16), :], fg.at[2 * mem + m],
                   fc_s.at[m], fc_r.at[m], member_peer(to)).start()
        sent(fg.at[0:7], fc_s.at[m], fc_r.at[m])
        fg[2 * mem + m] = f3[m, my_rows, :]

    hid_forward(0)
    hid_send(1)
    for m in range(2):
        received(fg.at[0:7], fc_s.at[m], fc_r.at[m])

    spread = (1.0 - (1.0 - ALPHA) / MEMBERS) / (MEMBERS * (MEMBERS - 1))
    soft = SOFTENING * SOFTENING
    truth_rows = truthp[my_rows, :]
    weight = wts[my_rows, :]

    def loss(k):
        to = rem(mem + k, 8)
        for i in range(2):
            f = fg[2 * to + i]
            gap = f[None] - fg[...]
            slopes = jnp.sum(gap * lax.rsqrt(gap * gap + soft), axis=0)
            off = f - truth_rows
            slope = off * lax.rsqrt(off * off + soft)
            lloc[2 * to + i] = (weight * (slope * (1.0 / MEMBERS) - spread * slopes)).astype(BF)

    for part in ((4, 3, 5), (2, 6, 1), (7, 0)):
        for k in part:
            loss(k)
        for k in part:
            if k:
                to = rem(mem + k, 8)
                remote(lloc.at[pl.ds(2 * to, 2)], l4.at[:, mem], lg_s, lg_r, member_peer(to)).start()
    sent(lloc.at[0:14], lg_s, lg_r)
    hid_forward(1)
    hid_send(2)
    for m in range(2):
        l4[m, mem] = lloc[2 * mem + m]
    received(lloc.at[0:14], lg_s, lg_r)

    for m in range(2):
        grad = l4[m].reshape(128, 256)
        for i in range(4):
            rows = slice(256 * i, 256 * i + 256)
            ug[m, rows, :] = mm(headp[rows, :], grad).astype(BF)
    low = (lane_of < 64)[0:64]
    order = (2, 1, 3, 0)

    def back_copy(h, step, d, inward=False):
        side = d if inward else 1 - d
        return remote(nsend.at[d, h, step], nrecv.at[h, step, side], nh_s.at[h, step, d],
                      nh_r.at[h, step, side], (below, above)[d])

    def keep(h, step, i, m, both):
        cols = slice(128 * i, 128 * i + 128)
        nown[h, step, 64 * m:64 * m + 64, cols] = jnp.where(low, both[0:64], both[64:128])
        halo_part = jnp.where(low, both[128:192], both[192:256]).astype(BF)
        nsend[0, h, step, m, :, cols] = halo_part[0:32]
        nsend[1, h, step, m, :, cols] = halo_part[32:64]

    def send_back(h, step):
        for d in range(2):
            copy = back_copy(h, step, d)
            copy.start()
            pending.append(copy)

    def merged_grad(step):
        rows = pl.ds(pl.multiple_of(rem(z + order[step], 4) * 256, 256), 256)
        for m in range(2):
            dm[step, m] = mm(ow[rows, :], ug[m]).astype(BF)

    merged_grad(0)
    for step in range(4):
        for i in range(2):
            for m in range(2):
                p = 2 * rem(z + order[step], 4) + i
                keep(0, step, i, m, mm(gt[m, p], dm[step, m, 128 * i:128 * i + 128, :], NT))
        if step < 3:
            merged_grad(step + 1)
        send_back(0, step)

    def score_grads(step):
        grads = []
        for i in range(2):
            for m in range(2):
                p = 2 * rem(z + order[step], 4) + i
                value = jnp.concatenate([by_head(kvo[8 + p, 64 * m:64 * m + 64, :]),
                                         by_head(kvh[8 + p, 64 * m:64 * m + 64, :])], axis=0)
                gate_grad = mm(value, dm[step, m, 128 * i:128 * i + 128, :])
                grads.append((gate_grad * dsg[m, p]).astype(BF))
        return grads

    ready = score_grads(0)

    for a in range(2):
        for i in range(4):
            rows = slice(1024 * a + 256 * i, 1024 * a + 256 * i + 256)
            both = mm(um[0, rows, :], l4[0].reshape(128, 256), NT) + mm(
                um[1, rows, :], l4[1].reshape(128, 256), NT)
            ah[i % 2, a, i // 2] = both.astype(BF)
    swap = remote(ah.at[1 - core], ahx, ax_s, ax_r, sibling)
    swap.start()
    hid_forward(2)
    pending.append(swap)

    for step in range(4):
        for i in range(2):
            for m in range(2):
                p = 2 * rem(z + order[step], 4) + i
                keep(1, step, i, m, mm(ready[2 * i + m], q3[p]))
        if step < 3:
            ready = score_grads(step + 1)
        send_back(1, step)

    def node_step(h, step):
        g = rem(z + order[step], 4)
        for d in range(2):
            back_copy(h, step, d, True).wait_recv()
        total = (nown[h, step] + mm(scatter, nrecv[h, step].reshape(128, 256))).astype(BF)
        for c in range(2):
            nsnd[h, step, c] = total[:, 128 * c:128 * c + 128]
        if step < 3:
            for c in range(2):
                remote(nsnd.at[h, step, c], nrcv.at[h, group], na_s.at[h], na_r.at[h],
                       group_peer(2 * g + c)).start()
        else:
            remote(nsnd.at[h, 3, 1 - core], nrcv.at[h, group], na_s.at[h], na_r.at[h], sibling).start()
            sent(nrcv.at[h, 0:7], na_s.at[h], na_r.at[h])
            nrcv[h, group] = nsnd[h, 3, core]
        nt[:, pl.ds(pl.multiple_of(1024 * (1 - h) + g * 256, 256), 256)] = total

    swap.wait_recv()
    for a in range(2):
        for i in range(2):
            both = ah[core, a, i].astype(F32) + ahx[a, i].astype(F32)
            both = both.astype(BF).reshape(2, 4, 2, 16, 128)
            for to in range(4):
                ahs[to, a, i] = both[:, to]
    for k in (2, 1, 3):
        to = rem(x + k, 4)
        remote(ahs.at[to], ahr.at[x], ah_s, ah_r, (mem, band + 4 * (to - x))).start()
    sent(ahr.at[0:3], ah_s, ah_r)
    ahr[x] = ahs[x]

    for step in range(4):
        node_step(0, step)


    for step in range(4):
        node_step(1, step)

    received(ahr.at[0:3], ah_s, ah_r)
    both = jnp.sum(ahr[...].astype(F32), axis=0).astype(BF)
    for to in range(4):
        ahs2[to] = both[:, :, to % 2, to // 2]
    for k in range(1, 4):
        to = rem(y + k, 4)
        remote(ahs2.at[to], ahr2.at[y], ay_s, ay_r,
               (z * 2 + rem(to, 2), x * 4 + div(to, 2) * 2 + core)).start()
    sent(ahr2.at[0:3], ay_s, ay_r)
    ahr2[y] = ahs2[y]

    received(hgt.at[0], sib_s.at[3], sib_r.at[3])
    for a in range(3):
        received(hid_bulk(a), sib_s.at[a], sib_r.at[a])
    for h in range(2):
        received(nrcv.at[h, 0:7], na_s.at[h], na_r.at[h])
        node_cols = nrcv[h].reshape(1024, 128)
        for i in range(4):
            rows = slice(256 * i, 256 * i + 256)
            left = jnp.concatenate([hgt[j, rows, :] for j in range(8)], axis=1)
            kvp[h, :, i] = mm(left, node_cols).astype(BF).reshape(16, 16, 128)
        for k in range(1, 16):
            to = rem(plane + k, 16)
            remote(kvp.at[h, to], kvr.at[h, plane], rs_s.at[h], rs_r.at[h], plane_peer(to)).start()
        kvr[h, plane] = kvp[h, plane]

    for i in range(4):
        rows = slice(256 * i, 256 * i + 256)
        hg[:, rows] = mm(nt[...], kvw[rows, :], NT)
    hg_copy = pltpu.make_async_copy(hg, hg_hbm, out_sem)
    hg_copy.start()
    flush()

    def fin_send(part, sem):
        for k in (4, 5, 2, 3, 6, 7, 1):
            to = rem(group + k, 8)
            remote(fsnd.at[part, to], frcv.at[part, group], fin_s.at[sem], fin_r.at[sem],
                   group_peer(to)).start()
        bulk = frcv.at[part, 0:7]
        sent(bulk, fin_s.at[sem], fin_r.at[sem])

    received(ahr2.at[0:3], ay_s, ay_r)
    ah_sum = jnp.sum(ahr2[...].astype(F32), axis=0)
    for i in range(2):
        for c in range(2):
            at = (2 * i + core) * 2 + c
            other = (2 * i + 1 - core) * 2 + c
            for a in range(2):
                fsnd[2 + a, at] = ah_sum[a, i, 8 * c:8 * c + 8]
                fsnd[2 + a, other] = jnp.zeros((8, 128), F32)
    for part in (2, 3):
        fin_send(part, part)
        frcv[part, group] = fsnd[part, group]
    for h in range(2):
        received(kvr.at[h, 0:15], rs_s.at[h], rs_r.at[h])
        fsnd[h] = jnp.sum(kvr[h].astype(F32), axis=0).reshape(8, 8, 128)
        fin_send(h, h)
        frcv[h, group] = fsnd[h, group]
    for h in range(2):
        sent(kvr.at[h, 0:15], rs_s.at[h], rs_r.at[h])
    flush()
    hg_copy.wait()
    for part in (2, 3, 0, 1):
        received(frcv.at[part, 0:7], fin_s.at[part], fin_r.at[part])


def finish(hg, frcv, head, hg_out, kv_out, og_out, hd_out, headt, sem):
    copy = pltpu.make_async_copy(hg, hg_out, sem)
    copy.start()
    headt[...] = jnp.zeros_like(headt)
    headt[0:100, :] = head[...]
    for j in range(8):
        at = 128 * j
        kv_out[:, at:at + 128] = frcv[1, j] * (1.0 / DEVICES)
        kv_out[:, 1024 + at:1024 + at + 128] = frcv[0, j] * (1.0 / DEVICES)
    sums = jnp.sum(frcv[2:4], axis=1) * (1.0 / DEVICES)
    hd_out[...] = sums[1, :, 0:100]
    outer = sums[0]
    big = outer.astype(BF)
    small = (outer - big.astype(F32)).astype(BF)
    og_out[...] = mm(big, headt[...]) + mm(small, headt[...])
    copy.wait()


def shards(hidden, queries, kv_weight, out_weight, head_projection, initial_state, truth,
           latitude_weight, channel_loss_weight, sources, halo_rows):
    vmem = pl.BlockSpec(memory_space=pltpu.VMEM)
    hbm = pl.BlockSpec(memory_space=pl.ANY)
    dma = pltpu.SemaphoreType.DMA
    scratch = [
        ((100, 1024), BF), ((100, 256), F32), ((100, 256), F32), ((1, 256), F32), ((1, 100), F32),
        ((3, 256), jnp.int32), ((2, 32), jnp.int32),
        ((2, 4, 32, 1024), BF), ((8, 256, 128), BF), ((1024, 2048), BF), ((1024, 1024), BF),
        ((1024, 1024), BF), ((1024, 256), BF), ((1024, 128), BF), ((128, 1024), BF),
        ((8, 1024, 128), BF), ((2, 2, 32, 1024), BF), ((8, 128), jnp.int32), ((16, 128, 128), BF),
        ((16, 128, 128), BF), ((2, 8, 128, 128), BF),
        ((256, 256), F32), ((2, 8, 256, 256), BF), ((2, 8, 256, 256), F32), ((2, 2048, 256), BF),
        ((128, 256), F32), ((128, 256), F32), ((128, 256), F32), ((2, 128, 256), F32),
        ((16, 16, 256), F32), ((16, 16, 256), BF), ((2, 8, 16, 256), BF), ((2, 1024, 256), BF),
        ((4, 2, 256, 256), BF), ((2, 2, 2, 256, 128), BF), ((2, 2, 256, 128), BF),
        ((4, 2, 2, 2, 2, 16, 128), BF), ((4, 2, 2, 2, 2, 16, 128), BF),
        ((4, 2, 2, 16, 128), BF), ((4, 2, 2, 16, 128), BF),
        ((2, 4, 128, 256), F32), ((2, 2, 4, 2, 32, 256), BF), ((2, 4, 2, 2, 32, 256), BF),
        ((128, 2048), BF), ((2, 4, 2, 128, 128), BF), ((2, 8, 128, 128), BF),
        ((2, 16, 4, 16, 128), BF), ((2, 16, 4, 16, 128), BF), ((4, 8, 8, 128), F32),
        ((128, 1024), F32),
    ]
    sems = [(18,), (), (2,), (2,), (3,), (3,), (4,), (4,), (2,), (2,), (), (), (), (), (), (), (2, 4, 2),
            (2, 4, 2), (2,), (2,), (2,), (2,), (4,), (4,), (), ()]
    raw_hidden, raw_sums = pl.pallas_call(
        body,
        out_shape=[jax.ShapeDtypeStruct((128, 1024), F32), jax.ShapeDtypeStruct((4, 8, 8, 128), F32)],
        in_specs=[hbm] * 11,
        out_specs=[hbm, vmem],
        scratch_shapes=[pltpu.VMEM(shape, kind) for shape, kind in scratch] + [dma(n) for n in sems],
        compiler_params=pltpu.CompilerParams(
            collective_id=0, has_side_effects=True, vmem_limit_bytes=56 * 1024 * 1024),
    )(
        hidden.reshape(2, 2, 32, 1024), queries, kv_weight, out_weight, head_projection.T,
        initial_state, truth, latitude_weight.reshape(1, 256), channel_loss_weight.reshape(1, 100),
        sources, halo_rows,
    )
    hidden_grad, kv_grad, out_grad, head_grad = pl.pallas_call(
        finish,
        out_shape=[jax.ShapeDtypeStruct((128, 1024), F32), jax.ShapeDtypeStruct((8, 2048), F32),
                   jax.ShapeDtypeStruct((8, 1024), F32), jax.ShapeDtypeStruct((8, 100), F32)],
        in_specs=[vmem, vmem, vmem],
        out_specs=[hbm, vmem, vmem, vmem],
        scratch_shapes=[pltpu.VMEM((128, 1024), BF), dma(())],
    )(raw_hidden, raw_sums, head_projection.T)
    return hidden_grad.reshape(2, 64, 1024), kv_grad, out_grad, head_grad


def solution(mesh):
    placed = (
        P("member", "band", None),
        P("band", None),
        P(),
        P(),
        P(),
        P(None, "band"),
        P(None, "band"),
        P("band"),
        P(),
        P(None, "band"),
        P("band", None),
    )
    return jax.shard_map(
        shards,
        mesh=mesh,
        in_specs=placed,
        out_specs=(
            P("member", "band", None),
            P(("member", "band"), None),
            P(("member", "band"), None),
            P(("member", "band"), None),
        ),
        check_vma=False,
    )
```

```python
import jax
import jax.numpy as jnp
from jax import lax
from jax.experimental import pallas as pl
from jax.experimental.pallas import tpu as pltpu
from jax.sharding import PartitionSpec as P

MESH = pl.DeviceIdType.MESH
BF = jnp.bfloat16
F32 = jnp.float32
ALPHA = 0.95
SOFTENING = 0.5
MEMBERS = 16
DEVICES = 128
NN = (((1,), (0,)), ((), ()))
NT = (((1,), (1,)), ((), ()))


def mm(a, b, dims=NN):
    return lax.dot_general(a, b, dims, preferred_element_type=F32)


def rem(a, n):
    return lax.rem(a, jnp.int32(n))


def div(a, n):
    return lax.div(a, jnp.int32(n))


def body(
    hid_hbm, q_hbm, kvw_hbm, ow_hbm, head_hbm, init_hbm, truth_hbm, lat_hbm, cw_hbm, src_hbm, halo_hbm,
    hg_hbm, frcv,
    head, init, truth, lat, cw, src, halo,
    ext, q3, kvw, ow, owt, qt, headp, headt, hgt, pick, lrow, kvo, kvh, vto, mask, gt, dsg, um,
    initp, truthp, wts, f3, fg, lloc, l4, ug, dm, ah, ahx, ahs, ahr, ahs2, ahr2, nown, nsend, nrecv, nt, nsnd,
    nrcv, kvp, kvr, fsnd, hg,
    in_sem, out_sem, halo_s, halo_r, hid_s, hid_r, sib_s, sib_r, fc_s, fc_r, lg_s, lg_r,
    ah_s, ah_r, ay_s, ay_r, nh_s, nh_r, na_s, na_r, rs_s, rs_r, fin_s, fin_r, ax_s, ax_r,
):
    mem, band = lax.axis_index("member"), lax.axis_index("band")
    z, ylo = div(mem, 2), rem(mem, 2)
    core = rem(band, 2)
    group = z * 2 + core
    plane = ylo * 8 + div(band, 2)
    x, yhi = div(band, 4), rem(div(band, 2), 2)
    y = yhi * 2 + ylo
    sibling = (mem, band + 1 - 2 * core)
    below, above = (mem, rem(band + 15, 16)), (mem, rem(band + 1, 16))
    pending = []

    def group_peer(j):
        return div(j, 2) * 2 + ylo, band - core + rem(j, 2)

    def plane_peer(q):
        return z * 2 + div(q, 8), rem(q, 8) * 2 + core

    def member_peer(m):
        return m, band

    def remote(source, target, send, recv, device):
        return pltpu.make_async_remote_copy(
            src_ref=source, dst_ref=target, send_sem=send, recv_sem=recv,
            device_id=device, device_id_type=MESH)

    def sent(bulk, send, recv):
        pending.append(remote(bulk, bulk, send, recv, sibling))

    def received(bulk, send, recv):
        remote(bulk, bulk, send, recv, sibling).wait_recv()

    def flush():
        while pending:
            pending.pop(0).wait_send()

    loads = [pltpu.make_async_copy(source, target, in_sem.at[i]) for i, (source, target) in enumerate([
        (halo_hbm, halo), (hid_hbm, ext.at[:, 0:2]), (src_hbm, src), (lat_hbm, lat), (cw_hbm, cw),
        (init_hbm, init), (truth_hbm, truth), (head_hbm, head), (ow_hbm, ow), (kvw_hbm, kvw)])]
    loads += [pltpu.make_async_copy(q_hbm.at[:, 128 * p:128 * p + 128], q3.at[p], in_sem.at[10 + p])
              for p in range(8)]
    loads[0].start()
    loads[1].start()

    barrier = pltpu.get_barrier_semaphore()

    def greet(device):
        pl.semaphore_signal(barrier, inc=1, device_id=device, device_id_type=MESH)

    for k in (10, 9, 11, 6, 5, 7, 8, 2, 13, 14, 3, 1, 15, 4, 12):
        greet(plane_peer(rem(plane + k, 16)))
    greet(below)
    greet(above)
    for k in range(4):
        greet(member_peer(rem(mem + 2 * k + 1, 8)))
    for k in range(1, 8):
        greet(group_peer(rem(group + k, 8)))

    loads[0].wait()
    for m in range(2):
        for d in range(2):
            at = 64 * d + 32 * m
            lrow[0:1, at:at + 32] = halo[d:d + 1, :] + 64 * m
    row_of = lax.broadcasted_iota(jnp.int32, (128, 128), 0)
    lane_of = lax.broadcasted_iota(jnp.int32, (128, 128), 1)
    scatter = (row_of == lrow[0:1, :]).astype(F32)
    gather = scatter.T.astype(BF)
    scatter = scatter.astype(BF)

    loads[1].wait()
    for copy in loads[2:8] + loads[10:] + loads[8:10]:
        copy.start()
    own = ext[:, 0:2].reshape(128, 1024)
    for n in range(4):
        cols = slice(256 * n, 256 * n + 256)
        pick[:, :, :, cols] = mm(gather, own[:, cols]).astype(BF).reshape(2, 2, 32, 256)

    pl.semaphore_wait(barrier, 28)
    to_below = remote(pick.at[0], ext.at[:, 3], halo_s.at[0], halo_r.at[0], below)
    to_above = remote(pick.at[1], ext.at[:, 2], halo_s.at[1], halo_r.at[1], above)
    to_below.start()
    to_above.start()
    pending.extend([to_below, to_above])

    for n in range(8):
        rows = slice(128 * n, 128 * n + 128)
        hgt[group, rows, :] = own[:, rows].T
    pieces = (pl.ds(0, 256), pl.ds(256, 256), pl.ds(512, 512))

    def hid_piece(a, j):
        return hgt.at[j, pieces[a]]

    def hid_bulk(a):
        return hgt.at[0:3, pieces[a]]

    def hid_send(a):
        for k in (2, 1, 3):
            remote(hid_piece(a, group), hid_piece(a, group), hid_s.at[a], hid_r.at[a],
                   group_peer(rem(group + 2 * k, 8))).start()
        sent(hid_bulk(a), hid_s.at[a], hid_r.at[a])

    def hid_forward(a):
        received(hid_bulk(a), hid_s.at[a], hid_r.at[a])
        for k in (1, 2, 3):
            block = hid_piece(a, rem(group + 2 * k, 8))
            remote(block, block, sib_s.at[a], sib_r.at[a], sibling).start()
        sent(hid_bulk(a), sib_s.at[a], sib_r.at[a])

    hid_send(0)
    remote(hgt.at[group], hgt.at[group], sib_s.at[3], sib_r.at[3], sibling).start()
    sent(hgt.at[0], sib_s.at[3], sib_r.at[3])

    for copy in loads[2:8]:
        copy.wait()
    headt[...] = jnp.zeros_like(headt)
    headt[0:100, :] = head[...]
    headp[...] = headt[...].T
    initp[...] = jnp.zeros_like(initp)
    initp[0:100, :] = init[...]
    truthp[...] = jnp.zeros_like(truthp)
    truthp[0:100, :] = truth[...]
    wts[...] = jnp.zeros_like(wts)
    wts[0:1, 0:100] = cw[...]
    diag = jnp.where(row_of == lane_of, wts[0:1, 0:128], 0.0)
    wts[...] = jnp.sum(diag, axis=1, keepdims=True) * lat[...]
    point_row = lax.broadcasted_iota(jnp.int32, (128, 256), 0)
    edge = (point_row == src[0:1, :]) | (point_row == src[1:2, :]) | (point_row == src[2:3, :])
    edge = edge.astype(F32)
    for at in (0, 64):
        mask[at:at + 64, :] = edge[0:64]
        mask[128 + at:128 + at + 64, :] = edge[64:128]
    lo_lane = (lane_of < 64).astype(BF)[0:64]
    hi_lane = (lane_of >= 64).astype(BF)[0:64]
    for p in range(8):
        loads[10 + p].wait()
        qt[128 * p:128 * p + 128, :] = q3[p].T
    loads[8].wait()
    for i in range(4):
        rows = slice(256 * i, 256 * i + 256)
        for j in range(4):
            cols = slice(256 * j, 256 * j + 256)
            owt[rows, cols] = ow[cols, rows].T

    def project(rows, target):
        for n in range(8):
            part = mm(rows, kvw[:, 256 * n:256 * n + 256]).astype(BF)
            target[2 * n] = part[:, :128]
            target[2 * n + 1] = part[:, 128:]

    def by_head(block):
        return jnp.concatenate([block * lo_lane, block * hi_lane], axis=0)

    def gates(part, source, m, p):
        at = slice(128 * part, 128 * part + 128)
        score = mm(by_head(source[p, 64 * m:64 * m + 64, :]), q3[p], NT)
        th = jnp.tanh(score * (0.5 / 8.0))
        on = mask[at, :]
        gate = ((0.5 + 0.5 * th) * on).astype(BF)
        gt[m, p, at, :] = gate
        dsg[m, p, at, :] = (0.25 - 0.25 * th * th) * (on * 0.125)
        return gate

    loads[9].wait()
    project(own, kvo)
    for m in range(2):
        for p in range(8):
            gates(0, kvo, m, p)
            vto[m, p] = by_head(kvo[8 + p, 64 * m:64 * m + 64, :]).T
    to_below.wait_recv()
    to_above.wait_recv()
    project(ext[:, 2:4].reshape(128, 1024), kvh)

    my_rows = pl.ds(pl.multiple_of(mem * 16, 16), 16)
    for m in range(2):
        for p in range(8):
            gate = jnp.concatenate([gt[m, p, 0:128, :], gates(1, kvh, m, p)], axis=0)
            value = by_head(kvh[8 + p, 64 * m:64 * m + 64, :]).T
            value = jnp.concatenate([vto[m, p], value], axis=1)
            um[m, 128 * p:128 * p + 128, :] = mm(value, gate).astype(BF)
        merged = um[m, 0:1024, :]
        for i in range(4):
            rows = slice(256 * i, 256 * i + 256)
            up = mm(owt[rows, :], merged) + qt[rows, :].astype(F32)
            um[m, 1024 + 256 * i:1024 + 256 * i + 256, :] = up.astype(BF)
        f3[m] = mm(headt[...], um[m, 1024:2048, :]) + initp[...]
        for k in range(7, 0, -1):
            to = rem(mem + k, 8)
            remote(f3.at[m, pl.ds(pl.multiple_of(to * 16, 16), 16), :], fg.at[2 * mem + m],
                   fc_s.at[m], fc_r.at[m], member_peer(to)).start()
        sent(fg.at[0:7], fc_s.at[m], fc_r.at[m])
        fg[2 * mem + m] = f3[m, my_rows, :]

    hid_forward(0)
    hid_send(1)
    for m in range(2):
        received(fg.at[0:7], fc_s.at[m], fc_r.at[m])

    spread = (1.0 - (1.0 - ALPHA) / MEMBERS) / (MEMBERS * (MEMBERS - 1))
    soft = SOFTENING * SOFTENING
    truth_rows = truthp[my_rows, :]
    weight = wts[my_rows, :]

    def loss(k):
        to = rem(mem + k, 8)
        for i in range(2):
            f = fg[2 * to + i]
            gap = f[None] - fg[...]
            slopes = jnp.sum(gap * lax.rsqrt(gap * gap + soft), axis=0)
            off = f - truth_rows
            slope = off * lax.rsqrt(off * off + soft)
            lloc[2 * to + i] = (weight * (slope * (1.0 / MEMBERS) - spread * slopes)).astype(BF)

    for part in ((4, 3, 5), (2, 6, 1), (7, 0)):
        for k in part:
            loss(k)
        for k in part:
            if k:
                to = rem(mem + k, 8)
                remote(lloc.at[pl.ds(2 * to, 2)], l4.at[:, mem], lg_s, lg_r, member_peer(to)).start()
    sent(lloc.at[0:14], lg_s, lg_r)
    hid_forward(1)
    for m in range(2):
        l4[m, mem] = lloc[2 * mem + m]
    received(lloc.at[0:14], lg_s, lg_r)
    hid_send(2)

    for m in range(2):
        grad = l4[m].reshape(128, 256)
        for i in range(4):
            rows = slice(256 * i, 256 * i + 256)
            ug[m, rows, :] = mm(headp[rows, :], grad).astype(BF)
    low = (lane_of < 64)[0:64]
    order = (2, 1, 3, 0)

    def back_copy(h, step, d, inward=False):
        side = d if inward else 1 - d
        return remote(nsend.at[d, h, step], nrecv.at[h, step, side], nh_s.at[h, step, d],
                      nh_r.at[h, step, side], (below, above)[d])

    def keep(h, step, i, m, both):
        cols = slice(128 * i, 128 * i + 128)
        nown[h, step, 64 * m:64 * m + 64, cols] = jnp.where(low, both[0:64], both[64:128])
        halo_part = jnp.where(low, both[128:192], both[192:256]).astype(BF)
        nsend[0, h, step, m, :, cols] = halo_part[0:32]
        nsend[1, h, step, m, :, cols] = halo_part[32:64]

    def send_back(h, step):
        for d in range(2):
            copy = back_copy(h, step, d)
            copy.start()
            pending.append(copy)

    def merged_grad(step):
        rows = pl.ds(pl.multiple_of(rem(z + order[step], 4) * 256, 256), 256)
        for m in range(2):
            dm[step, m] = mm(ow[rows, :], ug[m]).astype(BF)

    merged_grad(0)
    for step in range(4):
        for i in range(2):
            for m in range(2):
                p = 2 * rem(z + order[step], 4) + i
                keep(0, step, i, m, mm(gt[m, p], dm[step, m, 128 * i:128 * i + 128, :], NT))
        if step < 3:
            merged_grad(step + 1)
        send_back(0, step)

    def score_grads(step):
        grads = []
        for i in range(2):
            for m in range(2):
                p = 2 * rem(z + order[step], 4) + i
                value = jnp.concatenate([by_head(kvo[8 + p, 64 * m:64 * m + 64, :]),
                                         by_head(kvh[8 + p, 64 * m:64 * m + 64, :])], axis=0)
                gate_grad = mm(value, dm[step, m, 128 * i:128 * i + 128, :])
                grads.append((gate_grad * dsg[m, p]).astype(BF))
        return grads

    ready = score_grads(0)

    for a in range(2):
        for i in range(4):
            rows = slice(1024 * a + 256 * i, 1024 * a + 256 * i + 256)
            both = mm(um[0, rows, :], l4[0].reshape(128, 256), NT) + mm(
                um[1, rows, :], l4[1].reshape(128, 256), NT)
            ah[i % 2, a, i // 2] = both.astype(BF)
    swap = remote(ah.at[1 - core], ahx, ax_s, ax_r, sibling)
    swap.start()
    pending.append(swap)

    for step in range(4):
        for i in range(2):
            for m in range(2):
                p = 2 * rem(z + order[step], 4) + i
                keep(1, step, i, m, mm(ready[2 * i + m], q3[p]))
        if step < 3:
            ready = score_grads(step + 1)
        send_back(1, step)

    def node_step(h, step):
        g = rem(z + order[step], 4)
        for d in range(2):
            back_copy(h, step, d, True).wait_recv()
        total = (nown[h, step] + mm(scatter, nrecv[h, step].reshape(128, 256))).astype(BF)
        for c in range(2):
            nsnd[h, step, c] = total[:, 128 * c:128 * c + 128]
        if step < 3:
            for c in range(2):
                remote(nsnd.at[h, step, c], nrcv.at[h, group], na_s.at[h], na_r.at[h],
                       group_peer(2 * g + c)).start()
        else:
            remote(nsnd.at[h, 3, 1 - core], nrcv.at[h, group], na_s.at[h], na_r.at[h], sibling).start()
            sent(nrcv.at[h, 0:7], na_s.at[h], na_r.at[h])
            nrcv[h, group] = nsnd[h, 3, core]
        nt[:, pl.ds(pl.multiple_of(1024 * (1 - h) + g * 256, 256), 256)] = total

    swap.wait_recv()
    for a in range(2):
        for i in range(2):
            both = ah[core, a, i].astype(F32) + ahx[a, i].astype(F32)
            both = both.astype(BF).reshape(2, 4, 2, 16, 128)
            for to in range(4):
                ahs[to, a, i] = both[:, to]
    for k in (2, 1, 3):
        to = rem(x + k, 4)
        remote(ahs.at[to], ahr.at[x], ah_s, ah_r, (mem, band + 4 * (to - x))).start()
    sent(ahr.at[0:3], ah_s, ah_r)
    ahr[x] = ahs[x]

    for step in range(4):
        node_step(0, step)
    hid_forward(2)


    for step in range(4):
        node_step(1, step)

    received(hgt.at[0], sib_s.at[3], sib_r.at[3])
    for a in range(3):
        received(hid_bulk(a), sib_s.at[a], sib_r.at[a])
    for h in range(2):
        received(nrcv.at[h, 0:7], na_s.at[h], na_r.at[h])
        node_cols = nrcv[h].reshape(1024, 128)
        for i in range(4):
            rows = slice(256 * i, 256 * i + 256)
            left = jnp.concatenate([hgt[j, rows, :] for j in range(8)], axis=1)
            kvp[h, :, i] = mm(left, node_cols).astype(BF).reshape(16, 16, 128)
        for k in range(1, 16):
            to = rem(plane + k, 16)
            remote(kvp.at[h, to], kvr.at[h, plane], rs_s.at[h], rs_r.at[h], plane_peer(to)).start()
        kvr[h, plane] = kvp[h, plane]
        if h:
            continue
        received(ahr.at[0:3], ah_s, ah_r)
        both = jnp.sum(ahr[...].astype(F32), axis=0).astype(BF)
        for to in range(4):
            ahs2[to] = both[:, :, to % 2, to // 2]
        for k in range(1, 4):
            to = rem(y + k, 4)
            remote(ahs2.at[to], ahr2.at[y], ay_s, ay_r,
                   (z * 2 + rem(to, 2), x * 4 + div(to, 2) * 2 + core)).start()
        sent(ahr2.at[0:3], ay_s, ay_r)
        ahr2[y] = ahs2[y]

    for i in range(4):
        rows = slice(256 * i, 256 * i + 256)
        hg[:, rows] = mm(nt[...], kvw[rows, :], NT)
    hg_copy = pltpu.make_async_copy(hg, hg_hbm, out_sem)
    hg_copy.start()
    flush()

    def fin_send(part, sem):
        for k in (4, 5, 2, 3, 6, 7, 1):
            to = rem(group + k, 8)
            remote(fsnd.at[part, to], frcv.at[part, group], fin_s.at[sem], fin_r.at[sem],
                   group_peer(to)).start()
        bulk = frcv.at[part, 0:7]
        sent(bulk, fin_s.at[sem], fin_r.at[sem])

    received(ahr2.at[0:3], ay_s, ay_r)
    ah_sum = jnp.sum(ahr2[...].astype(F32), axis=0)
    for i in range(2):
        for c in range(2):
            at = (2 * i + core) * 2 + c
            other = (2 * i + 1 - core) * 2 + c
            for a in range(2):
                fsnd[2 + a, at] = ah_sum[a, i, 8 * c:8 * c + 8]
                fsnd[2 + a, other] = jnp.zeros((8, 128), F32)
    for part in (2, 3):
        fin_send(part, part)
        frcv[part, group] = fsnd[part, group]
    for h in range(2):
        received(kvr.at[h, 0:15], rs_s.at[h], rs_r.at[h])
        fsnd[h] = jnp.sum(kvr[h].astype(F32), axis=0).reshape(8, 8, 128)
        fin_send(h, h)
        frcv[h, group] = fsnd[h, group]
    for h in range(2):
        sent(kvr.at[h, 0:15], rs_s.at[h], rs_r.at[h])
    flush()
    hg_copy.wait()
    for part in (2, 3, 0, 1):
        received(frcv.at[part, 0:7], fin_s.at[part], fin_r.at[part])


def finish(hg, frcv, head, hg_out, kv_out, og_out, hd_out, headt, sem):
    copy = pltpu.make_async_copy(hg, hg_out, sem)
    copy.start()
    headt[...] = jnp.zeros_like(headt)
    headt[0:100, :] = head[...]
    for j in range(8):
        at = 128 * j
        kv_out[:, at:at + 128] = frcv[1, j] * (1.0 / DEVICES)
        kv_out[:, 1024 + at:1024 + at + 128] = frcv[0, j] * (1.0 / DEVICES)
    sums = jnp.sum(frcv[2:4], axis=1) * (1.0 / DEVICES)
    hd_out[...] = sums[1, :, 0:100]
    outer = sums[0]
    big = outer.astype(BF)
    small = (outer - big.astype(F32)).astype(BF)
    og_out[...] = mm(big, headt[...]) + mm(small, headt[...])
    copy.wait()


def shards(hidden, queries, kv_weight, out_weight, head_projection, initial_state, truth,
           latitude_weight, channel_loss_weight, sources, halo_rows):
    vmem = pl.BlockSpec(memory_space=pltpu.VMEM)
    hbm = pl.BlockSpec(memory_space=pl.ANY)
    dma = pltpu.SemaphoreType.DMA
    scratch = [
        ((100, 1024), BF), ((100, 256), F32), ((100, 256), F32), ((1, 256), F32), ((1, 100), F32),
        ((3, 256), jnp.int32), ((2, 32), jnp.int32),
        ((2, 4, 32, 1024), BF), ((8, 256, 128), BF), ((1024, 2048), BF), ((1024, 1024), BF),
        ((1024, 1024), BF), ((1024, 256), BF), ((1024, 128), BF), ((128, 1024), BF),
        ((8, 1024, 128), BF), ((2, 2, 32, 1024), BF), ((8, 128), jnp.int32), ((16, 128, 128), BF),
        ((16, 128, 128), BF), ((2, 8, 128, 128), BF),
        ((256, 256), F32), ((2, 8, 256, 256), BF), ((2, 8, 256, 256), F32), ((2, 2048, 256), BF),
        ((128, 256), F32), ((128, 256), F32), ((128, 256), F32), ((2, 128, 256), F32),
        ((16, 16, 256), F32), ((16, 16, 256), BF), ((2, 8, 16, 256), BF), ((2, 1024, 256), BF),
        ((4, 2, 256, 256), BF), ((2, 2, 2, 256, 128), BF), ((2, 2, 256, 128), BF),
        ((4, 2, 2, 2, 2, 16, 128), BF), ((4, 2, 2, 2, 2, 16, 128), BF),
        ((4, 2, 2, 16, 128), BF), ((4, 2, 2, 16, 128), BF),
        ((2, 4, 128, 256), F32), ((2, 2, 4, 2, 32, 256), BF), ((2, 4, 2, 2, 32, 256), BF),
        ((128, 2048), BF), ((2, 4, 2, 128, 128), BF), ((2, 8, 128, 128), BF),
        ((2, 16, 4, 16, 128), BF), ((2, 16, 4, 16, 128), BF), ((4, 8, 8, 128), F32),
        ((128, 1024), F32),
    ]
    sems = [(18,), (), (2,), (2,), (3,), (3,), (4,), (4,), (2,), (2,), (), (), (), (), (), (), (2, 4, 2),
            (2, 4, 2), (2,), (2,), (2,), (2,), (4,), (4,), (), ()]
    raw_hidden, raw_sums = pl.pallas_call(
        body,
        out_shape=[jax.ShapeDtypeStruct((128, 1024), F32), jax.ShapeDtypeStruct((4, 8, 8, 128), F32)],
        in_specs=[hbm] * 11,
        out_specs=[hbm, vmem],
        scratch_shapes=[pltpu.VMEM(shape, kind) for shape, kind in scratch] + [dma(n) for n in sems],
        compiler_params=pltpu.CompilerParams(
            collective_id=0, has_side_effects=True, vmem_limit_bytes=56 * 1024 * 1024),
    )(
        hidden.reshape(2, 2, 32, 1024), queries, kv_weight, out_weight, head_projection.T,
        initial_state, truth, latitude_weight.reshape(1, 256), channel_loss_weight.reshape(1, 100),
        sources, halo_rows,
    )
    hidden_grad, kv_grad, out_grad, head_grad = pl.pallas_call(
        finish,
        out_shape=[jax.ShapeDtypeStruct((128, 1024), F32), jax.ShapeDtypeStruct((8, 2048), F32),
                   jax.ShapeDtypeStruct((8, 1024), F32), jax.ShapeDtypeStruct((8, 100), F32)],
        in_specs=[vmem, vmem, vmem],
        out_specs=[hbm, vmem, vmem, vmem],
        scratch_shapes=[pltpu.VMEM((128, 1024), BF), dma(())],
    )(raw_hidden, raw_sums, head_projection.T)
    return hidden_grad.reshape(2, 64, 1024), kv_grad, out_grad, head_grad


def solution(mesh):
    placed = (
        P("member", "band", None),
        P("band", None),
        P(),
        P(),
        P(),
        P(None, "band"),
        P(None, "band"),
        P("band"),
        P(),
        P(None, "band"),
        P("band", None),
    )
    return jax.shard_map(
        shards,
        mesh=mesh,
        in_specs=placed,
        out_specs=(
            P("member", "band", None),
            P(("member", "band"), None),
            P(("member", "band"), None),
            P(("member", "band"), None),
        ),
        check_vma=False,
    )
```

```python
import jax
import jax.numpy as jnp
from jax import lax
from jax.experimental import pallas as pl
from jax.experimental.pallas import tpu as pltpu
from jax.sharding import PartitionSpec as P

MESH = pl.DeviceIdType.MESH
BF = jnp.bfloat16
F32 = jnp.float32
ALPHA = 0.95
SOFTENING = 0.5
MEMBERS = 16
DEVICES = 128
NN = (((1,), (0,)), ((), ()))
NT = (((1,), (1,)), ((), ()))


def mm(a, b, dims=NN):
    return lax.dot_general(a, b, dims, preferred_element_type=F32)


def rem(a, n):
    return lax.rem(a, jnp.int32(n))


def div(a, n):
    return lax.div(a, jnp.int32(n))


def body(
    hid_hbm, q_hbm, kvw_hbm, ow_hbm, head_hbm, init_hbm, truth_hbm, lat_hbm, cw_hbm, src_hbm, halo_hbm,
    hg_hbm, frcv,
    head, init, truth, lat, cw, src, halo,
    ext, q3, kvw, ow, owt, qt, headp, headt, hgt, pick, lrow, kvo, kvh, vto, mask, gt, dsg, um,
    initp, truthp, wts, f3, fg, lloc, l4, ug, dm, ah, ahx, ahs, ahr, ahs2, ahr2, nown, nsend, nrecv, nt, nsnd,
    nrcv, kvp, kvr, fsnd, hg,
    in_sem, out_sem, halo_s, halo_r, hid_s, hid_r, sib_s, sib_r, fc_s, fc_r, lg_s, lg_r,
    ah_s, ah_r, ay_s, ay_r, nh_s, nh_r, na_s, na_r, rs_s, rs_r, fin_s, fin_r, ax_s, ax_r,
):
    mem, band = lax.axis_index("member"), lax.axis_index("band")
    z, ylo = div(mem, 2), rem(mem, 2)
    core = rem(band, 2)
    group = z * 2 + core
    plane = ylo * 8 + div(band, 2)
    x, yhi = div(band, 4), rem(div(band, 2), 2)
    y = yhi * 2 + ylo
    sibling = (mem, band + 1 - 2 * core)
    below, above = (mem, rem(band + 15, 16)), (mem, rem(band + 1, 16))
    pending = []

    def group_peer(j):
        return div(j, 2) * 2 + ylo, band - core + rem(j, 2)

    def plane_peer(q):
        return z * 2 + div(q, 8), rem(q, 8) * 2 + core

    def member_peer(m):
        return m, band

    def remote(source, target, send, recv, device):
        return pltpu.make_async_remote_copy(
            src_ref=source, dst_ref=target, send_sem=send, recv_sem=recv,
            device_id=device, device_id_type=MESH)

    def sent(bulk, send, recv):
        pending.append(remote(bulk, bulk, send, recv, sibling))

    def received(bulk, send, recv):
        remote(bulk, bulk, send, recv, sibling).wait_recv()

    def flush():
        while pending:
            pending.pop(0).wait_send()

    loads = [pltpu.make_async_copy(source, target, in_sem.at[i]) for i, (source, target) in enumerate([
        (halo_hbm, halo), (hid_hbm, ext.at[:, 0:2]), (src_hbm, src), (lat_hbm, lat), (cw_hbm, cw),
        (init_hbm, init), (truth_hbm, truth), (head_hbm, head), (ow_hbm, ow), (kvw_hbm, kvw)])]
    loads += [pltpu.make_async_copy(q_hbm.at[:, 128 * p:128 * p + 128], q3.at[p], in_sem.at[10 + p])
              for p in range(8)]
    loads[0].start()
    loads[1].start()

    barrier = pltpu.get_barrier_semaphore()

    def greet(device):
        pl.semaphore_signal(barrier, inc=1, device_id=device, device_id_type=MESH)

    for k in (10, 9, 11, 6, 5, 7, 8, 2, 13, 14, 3, 1, 15, 4, 12):
        greet(plane_peer(rem(plane + k, 16)))
    greet(below)
    greet(above)
    for k in range(4):
        greet(member_peer(rem(mem + 2 * k + 1, 8)))
    for k in range(1, 8):
        greet(group_peer(rem(group + k, 8)))

    loads[0].wait()
    for m in range(2):
        for d in range(2):
            at = 64 * d + 32 * m
            lrow[0:1, at:at + 32] = halo[d:d + 1, :] + 64 * m
    row_of = lax.broadcasted_iota(jnp.int32, (128, 128), 0)
    lane_of = lax.broadcasted_iota(jnp.int32, (128, 128), 1)
    scatter = (row_of == lrow[0:1, :]).astype(F32)
    gather = scatter.T.astype(BF)
    scatter = scatter.astype(BF)

    loads[1].wait()
    for copy in loads[2:8] + loads[10:] + loads[8:10]:
        copy.start()
    own = ext[:, 0:2].reshape(128, 1024)
    for n in range(4):
        cols = slice(256 * n, 256 * n + 256)
        pick[:, :, :, cols] = mm(gather, own[:, cols]).astype(BF).reshape(2, 2, 32, 256)

    pl.semaphore_wait(barrier, 28)
    to_below = remote(pick.at[0], ext.at[:, 3], halo_s.at[0], halo_r.at[0], below)
    to_above = remote(pick.at[1], ext.at[:, 2], halo_s.at[1], halo_r.at[1], above)
    to_below.start()
    to_above.start()
    pending.extend([to_below, to_above])

    for n in range(8):
        rows = slice(128 * n, 128 * n + 128)
        hgt[group, rows, :] = own[:, rows].T
    pieces = (pl.ds(0, 256), pl.ds(256, 256), pl.ds(512, 512))

    def hid_piece(a, j):
        return hgt.at[j, pieces[a]]

    def hid_bulk(a):
        return hgt.at[0:3, pieces[a]]

    def hid_send(a):
        for k in (2, 1, 3):
            remote(hid_piece(a, group), hid_piece(a, group), hid_s.at[a], hid_r.at[a],
                   group_peer(rem(group + 2 * k, 8))).start()
        sent(hid_bulk(a), hid_s.at[a], hid_r.at[a])

    def hid_forward(a):
        received(hid_bulk(a), hid_s.at[a], hid_r.at[a])
        for k in (1, 2, 3):
            block = hid_piece(a, rem(group + 2 * k, 8))
            remote(block, block, sib_s.at[a], sib_r.at[a], sibling).start()
        sent(hid_bulk(a), sib_s.at[a], sib_r.at[a])

    hid_send(0)
    remote(hgt.at[group], hgt.at[group], sib_s.at[3], sib_r.at[3], sibling).start()
    sent(hgt.at[0], sib_s.at[3], sib_r.at[3])

    for copy in loads[2:8]:
        copy.wait()
    headt[...] = jnp.zeros_like(headt)
    headt[0:100, :] = head[...]
    headp[...] = headt[...].T
    initp[...] = jnp.zeros_like(initp)
    initp[0:100, :] = init[...]
    truthp[...] = jnp.zeros_like(truthp)
    truthp[0:100, :] = truth[...]
    wts[...] = jnp.zeros_like(wts)
    wts[0:1, 0:100] = cw[...]
    diag = jnp.where(row_of == lane_of, wts[0:1, 0:128], 0.0)
    wts[...] = jnp.sum(diag, axis=1, keepdims=True) * lat[...]
    point_row = lax.broadcasted_iota(jnp.int32, (128, 256), 0)
    edge = (point_row == src[0:1, :]) | (point_row == src[1:2, :]) | (point_row == src[2:3, :])
    edge = edge.astype(F32)
    for at in (0, 64):
        mask[at:at + 64, :] = edge[0:64]
        mask[128 + at:128 + at + 64, :] = edge[64:128]
    lo_lane = (lane_of < 64).astype(BF)[0:64]
    hi_lane = (lane_of >= 64).astype(BF)[0:64]
    for p in range(8):
        loads[10 + p].wait()
        qt[128 * p:128 * p + 128, :] = q3[p].T
    loads[8].wait()
    for i in range(4):
        rows = slice(256 * i, 256 * i + 256)
        for j in range(4):
            cols = slice(256 * j, 256 * j + 256)
            owt[rows, cols] = ow[cols, rows].T

    def project(rows, target):
        for n in range(8):
            part = mm(rows, kvw[:, 256 * n:256 * n + 256]).astype(BF)
            target[2 * n] = part[:, :128]
            target[2 * n + 1] = part[:, 128:]

    def by_head(block):
        return jnp.concatenate([block * lo_lane, block * hi_lane], axis=0)

    def gates(part, source, m, p):
        at = slice(128 * part, 128 * part + 128)
        score = mm(by_head(source[p, 64 * m:64 * m + 64, :]), q3[p], NT)
        th = jnp.tanh(score * (0.5 / 8.0))
        on = mask[at, :]
        gate = ((0.5 + 0.5 * th) * on).astype(BF)
        gt[m, p, at, :] = gate
        dsg[m, p, at, :] = (0.25 - 0.25 * th * th) * (on * 0.125)
        return gate

    loads[9].wait()
    project(own, kvo)
    for m in range(2):
        for p in range(8):
            gates(0, kvo, m, p)
            vto[m, p] = by_head(kvo[8 + p, 64 * m:64 * m + 64, :]).T
    to_below.wait_recv()
    to_above.wait_recv()
    project(ext[:, 2:4].reshape(128, 1024), kvh)

    my_rows = pl.ds(pl.multiple_of(mem * 16, 16), 16)
    for m in range(2):
        for p in range(8):
            gate = jnp.concatenate([gt[m, p, 0:128, :], gates(1, kvh, m, p)], axis=0)
            value = by_head(kvh[8 + p, 64 * m:64 * m + 64, :]).T
            value = jnp.concatenate([vto[m, p], value], axis=1)
            um[m, 128 * p:128 * p + 128, :] = mm(value, gate).astype(BF)
        merged = um[m, 0:1024, :]
        for i in range(4):
            rows = slice(256 * i, 256 * i + 256)
            up = mm(owt[rows, :], merged) + qt[rows, :].astype(F32)
            um[m, 1024 + 256 * i:1024 + 256 * i + 256, :] = up.astype(BF)
        f3[m] = mm(headt[...], um[m, 1024:2048, :]) + initp[...]
        for k in range(7, 0, -1):
            to = rem(mem + k, 8)
            remote(f3.at[m, pl.ds(pl.multiple_of(to * 16, 16), 16), :], fg.at[2 * mem + m],
                   fc_s.at[m], fc_r.at[m], member_peer(to)).start()
        sent(fg.at[0:7], fc_s.at[m], fc_r.at[m])
        fg[2 * mem + m] = f3[m, my_rows, :]

    hid_forward(0)
    hid_send(1)
    for m in range(2):
        received(fg.at[0:7], fc_s.at[m], fc_r.at[m])

    spread = (1.0 - (1.0 - ALPHA) / MEMBERS) / (MEMBERS * (MEMBERS - 1))
    soft = SOFTENING * SOFTENING
    truth_rows = truthp[my_rows, :]
    weight = wts[my_rows, :]

    def loss(k):
        to = rem(mem + k, 8)
        for i in range(2):
            f = fg[2 * to + i]
            gap = f[None] - fg[...]
            slopes = jnp.sum(gap * lax.rsqrt(gap * gap + soft), axis=0)
            off = f - truth_rows
            slope = off * lax.rsqrt(off * off + soft)
            lloc[2 * to + i] = (weight * (slope * (1.0 / MEMBERS) - spread * slopes)).astype(BF)

    for part in ((4, 3, 5), (2, 6, 1), (7, 0)):
        for k in part:
            loss(k)
        for k in part:
            if k:
                to = rem(mem + k, 8)
                remote(lloc.at[pl.ds(2 * to, 2)], l4.at[:, mem], lg_s, lg_r, member_peer(to)).start()
    sent(lloc.at[0:14], lg_s, lg_r)
    hid_forward(1)
    for m in range(2):
        l4[m, mem] = lloc[2 * mem + m]
    received(lloc.at[0:14], lg_s, lg_r)
    hid_send(2)

    for m in range(2):
        grad = l4[m].reshape(128, 256)
        for i in range(4):
            rows = slice(256 * i, 256 * i + 256)
            ug[m, rows, :] = mm(headp[rows, :], grad).astype(BF)
    low = (lane_of < 64)[0:64]
    order = (2, 1, 3, 0)

    def back_copy(h, step, d, inward=False):
        side = d if inward else 1 - d
        return remote(nsend.at[d, h, step], nrecv.at[h, step, side], nh_s.at[h, step, d],
                      nh_r.at[h, step, side], (below, above)[d])

    def keep(h, step, i, m, both):
        cols = slice(128 * i, 128 * i + 128)
        nown[h, step, 64 * m:64 * m + 64, cols] = jnp.where(low, both[0:64], both[64:128])
        halo_part = jnp.where(low, both[128:192], both[192:256]).astype(BF)
        nsend[0, h, step, m, :, cols] = halo_part[0:32]
        nsend[1, h, step, m, :, cols] = halo_part[32:64]

    def send_back(h, step):
        for d in range(2):
            copy = back_copy(h, step, d)
            copy.start()
            pending.append(copy)

    def merged_grad(step):
        rows = pl.ds(pl.multiple_of(rem(z + order[step], 4) * 256, 256), 256)
        for m in range(2):
            dm[step, m] = mm(ow[rows, :], ug[m]).astype(BF)

    merged_grad(0)
    for step in range(4):
        for i in range(2):
            for m in range(2):
                p = 2 * rem(z + order[step], 4) + i
                keep(0, step, i, m, mm(gt[m, p], dm[step, m, 128 * i:128 * i + 128, :], NT))
        if step < 3:
            merged_grad(step + 1)
        send_back(0, step)

    def score_grads(step):
        grads = []
        for i in range(2):
            for m in range(2):
                p = 2 * rem(z + order[step], 4) + i
                value = jnp.concatenate([by_head(kvo[8 + p, 64 * m:64 * m + 64, :]),
                                         by_head(kvh[8 + p, 64 * m:64 * m + 64, :])], axis=0)
                gate_grad = mm(value, dm[step, m, 128 * i:128 * i + 128, :])
                grads.append((gate_grad * dsg[m, p]).astype(BF))
        return grads

    ready = score_grads(0)

    for a in range(2):
        for i in range(4):
            rows = slice(1024 * a + 256 * i, 1024 * a + 256 * i + 256)
            both = mm(um[0, rows, :], l4[0].reshape(128, 256), NT) + mm(
                um[1, rows, :], l4[1].reshape(128, 256), NT)
            ah[i % 2, a, i // 2] = both.astype(BF)
    swap = remote(ah.at[1 - core], ahx, ax_s, ax_r, sibling)
    swap.start()
    pending.append(swap)

    for step in range(4):
        for i in range(2):
            for m in range(2):
                p = 2 * rem(z + order[step], 4) + i
                keep(1, step, i, m, mm(ready[2 * i + m], q3[p]))
        if step < 3:
            ready = score_grads(step + 1)
        send_back(1, step)

    def node_step(h, step):
        g = rem(z + order[step], 4)
        for d in range(2):
            back_copy(h, step, d, True).wait_recv()
        total = (nown[h, step] + mm(scatter, nrecv[h, step].reshape(128, 256))).astype(BF)
        for c in range(2):
            nsnd[h, step, c] = total[:, 128 * c:128 * c + 128]
        if step < 3:
            for c in range(2):
                remote(nsnd.at[h, step, c], nrcv.at[h, group], na_s.at[h], na_r.at[h],
                       group_peer(2 * g + c)).start()
        else:
            remote(nsnd.at[h, 3, 1 - core], nrcv.at[h, group], na_s.at[h], na_r.at[h], sibling).start()
            sent(nrcv.at[h, 0:7], na_s.at[h], na_r.at[h])
            nrcv[h, group] = nsnd[h, 3, core]
        nt[:, pl.ds(pl.multiple_of(1024 * (1 - h) + g * 256, 256), 256)] = total

    swap.wait_recv()
    for a in range(2):
        for i in range(2):
            both = ah[core, a, i].astype(F32) + ahx[a, i].astype(F32)
            both = both.astype(BF).reshape(2, 4, 2, 16, 128)
            for to in range(4):
                ahs[to, a, i] = both[:, to]
    for k in (2, 1, 3):
        to = rem(x + k, 4)
        remote(ahs.at[to], ahr.at[x], ah_s, ah_r, (mem, band + 4 * (to - x))).start()
    sent(ahr.at[0:3], ah_s, ah_r)
    ahr[x] = ahs[x]

    for step in range(4):
        node_step(0, step)
    hid_forward(2)


    for step in range(4):
        node_step(1, step)

    received(hgt.at[0], sib_s.at[3], sib_r.at[3])
    for a in range(3):
        received(hid_bulk(a), sib_s.at[a], sib_r.at[a])
    for h in range(2):
        received(nrcv.at[h, 0:7], na_s.at[h], na_r.at[h])
        node_cols = nrcv[h].reshape(1024, 128)
        for i in range(4):
            rows = slice(256 * i, 256 * i + 256)
            left = jnp.concatenate([hgt[j, rows, :] for j in range(8)], axis=1)
            kvp[h, :, i] = mm(left, node_cols).astype(BF).reshape(16, 16, 128)
        for k in range(1, 16):
            to = rem(plane + k, 16)
            remote(kvp.at[h, to], kvr.at[h, plane], rs_s.at[h], rs_r.at[h], plane_peer(to)).start()
        kvr[h, plane] = kvp[h, plane]
        if h:
            continue
        received(ahr.at[0:3], ah_s, ah_r)
        both = jnp.sum(ahr[...].astype(F32), axis=0).astype(BF)
        for to in range(4):
            ahs2[to] = both[:, :, to % 2, to // 2]
        for k in range(1, 4):
            to = rem(y + k, 4)
            remote(ahs2.at[to], ahr2.at[y], ay_s, ay_r,
                   (z * 2 + rem(to, 2), x * 4 + div(to, 2) * 2 + core)).start()
        sent(ahr2.at[0:3], ay_s, ay_r)
        ahr2[y] = ahs2[y]

    for i in range(4):
        rows = slice(256 * i, 256 * i + 256)
        hg[:, rows] = mm(nt[...], kvw[rows, :], NT)
    hg_copy = pltpu.make_async_copy(hg, hg_hbm, out_sem)
    hg_copy.start()
    flush()

    def fin_send(part, sem):
        for k in (4, 5, 2, 3, 6, 7, 1):
            to = rem(group + k, 8)
            remote(fsnd.at[part, to], frcv.at[part, group], fin_s.at[sem], fin_r.at[sem],
                   group_peer(to)).start()
        bulk = frcv.at[part, 0:7]
        sent(bulk, fin_s.at[sem], fin_r.at[sem])

    received(ahr2.at[0:3], ay_s, ay_r)
    ah_sum = jnp.sum(ahr2[...].astype(F32), axis=0)
    for i in range(2):
        for c in range(2):
            at = (2 * i + core) * 2 + c
            other = (2 * i + 1 - core) * 2 + c
            for a in range(2):
                fsnd[2 + a, at] = ah_sum[a, i, 8 * c:8 * c + 8]
                fsnd[2 + a, other] = jnp.zeros((8, 128), F32)
    for part in (2, 3):
        fin_send(part, part)
        frcv[part, group] = fsnd[part, group]
    for h in range(2):
        received(kvr.at[h, 0:15], rs_s.at[h], rs_r.at[h])
        fsnd[h] = jnp.sum(kvr[h].astype(F32), axis=0).reshape(8, 8, 128)
        fin_send(h, h)
        frcv[h, group] = fsnd[h, group]
    for h in range(2):
        sent(kvr.at[h, 0:15], rs_s.at[h], rs_r.at[h])
    flush()
    hg_copy.wait()
    for part in (2, 3, 0, 1):
        received(frcv.at[part, 0:7], fin_s.at[part], fin_r.at[part])


def finish(hg_hbm, frcv_hbm, head_hbm, hg_out, kv_out, og_out, hd_out, hg, frcv, head, headt, sem, out_sem):
    loads = [pltpu.make_async_copy(frcv_hbm, frcv, sem.at[4]),
             pltpu.make_async_copy(head_hbm, head, sem.at[5])]
    quarters = [pl.ds(32 * i, 32) for i in range(4)]
    loads += [pltpu.make_async_copy(hg_hbm.at[q], hg.at[q], sem.at[i]) for i, q in enumerate(quarters)]
    for copy in loads:
        copy.start()
    stores = [pltpu.make_async_copy(hg.at[q], hg_out.at[q], out_sem.at[i]) for i, q in enumerate(quarters)]
    headt[...] = jnp.zeros_like(headt)
    for load, store in zip(loads[2:], stores):
        load.wait()
        store.start()
    loads[0].wait()
    loads[1].wait()
    headt[0:100, :] = head[...]
    for j in range(8):
        at = 128 * j
        kv_out[:, at:at + 128] = frcv[1, j] * (1.0 / DEVICES)
        kv_out[:, 1024 + at:1024 + at + 128] = frcv[0, j] * (1.0 / DEVICES)
    sums = jnp.sum(frcv[2:4], axis=1) * (1.0 / DEVICES)
    hd_out[...] = sums[1, :, 0:100]
    outer = sums[0]
    big = outer.astype(BF)
    small = (outer - big.astype(F32)).astype(BF)
    og_out[...] = mm(big, headt[...]) + mm(small, headt[...])
    for copy in stores:
        copy.wait()


def shards(hidden, queries, kv_weight, out_weight, head_projection, initial_state, truth,
           latitude_weight, channel_loss_weight, sources, halo_rows):
    vmem = pl.BlockSpec(memory_space=pltpu.VMEM)
    hbm = pl.BlockSpec(memory_space=pl.ANY)
    dma = pltpu.SemaphoreType.DMA
    scratch = [
        ((100, 1024), BF), ((100, 256), F32), ((100, 256), F32), ((1, 256), F32), ((1, 100), F32),
        ((3, 256), jnp.int32), ((2, 32), jnp.int32),
        ((2, 4, 32, 1024), BF), ((8, 256, 128), BF), ((1024, 2048), BF), ((1024, 1024), BF),
        ((1024, 1024), BF), ((1024, 256), BF), ((1024, 128), BF), ((128, 1024), BF),
        ((8, 1024, 128), BF), ((2, 2, 32, 1024), BF), ((8, 128), jnp.int32), ((16, 128, 128), BF),
        ((16, 128, 128), BF), ((2, 8, 128, 128), BF),
        ((256, 256), F32), ((2, 8, 256, 256), BF), ((2, 8, 256, 256), F32), ((2, 2048, 256), BF),
        ((128, 256), F32), ((128, 256), F32), ((128, 256), F32), ((2, 128, 256), F32),
        ((16, 16, 256), F32), ((16, 16, 256), BF), ((2, 8, 16, 256), BF), ((2, 1024, 256), BF),
        ((4, 2, 256, 256), BF), ((2, 2, 2, 256, 128), BF), ((2, 2, 256, 128), BF),
        ((4, 2, 2, 2, 2, 16, 128), BF), ((4, 2, 2, 2, 2, 16, 128), BF),
        ((4, 2, 2, 16, 128), BF), ((4, 2, 2, 16, 128), BF),
        ((2, 4, 128, 256), F32), ((2, 2, 4, 2, 32, 256), BF), ((2, 4, 2, 2, 32, 256), BF),
        ((128, 2048), BF), ((2, 4, 2, 128, 128), BF), ((2, 8, 128, 128), BF),
        ((2, 16, 4, 16, 128), BF), ((2, 16, 4, 16, 128), BF), ((4, 8, 8, 128), F32),
        ((128, 1024), F32),
    ]
    sems = [(18,), (), (2,), (2,), (3,), (3,), (4,), (4,), (2,), (2,), (), (), (), (), (), (), (2, 4, 2),
            (2, 4, 2), (2,), (2,), (2,), (2,), (4,), (4,), (), ()]
    raw_hidden, raw_sums = pl.pallas_call(
        body,
        out_shape=[jax.ShapeDtypeStruct((128, 1024), F32), jax.ShapeDtypeStruct((4, 8, 8, 128), F32)],
        in_specs=[hbm] * 11,
        out_specs=[hbm, vmem],
        scratch_shapes=[pltpu.VMEM(shape, kind) for shape, kind in scratch] + [dma(n) for n in sems],
        compiler_params=pltpu.CompilerParams(
            collective_id=0, has_side_effects=True, vmem_limit_bytes=56 * 1024 * 1024),
    )(
        hidden.reshape(2, 2, 32, 1024), queries, kv_weight, out_weight, head_projection.T,
        initial_state, truth, latitude_weight.reshape(1, 256), channel_loss_weight.reshape(1, 100),
        sources, halo_rows,
    )
    hidden_grad, kv_grad, out_grad, head_grad = pl.pallas_call(
        finish,
        out_shape=[jax.ShapeDtypeStruct((128, 1024), F32), jax.ShapeDtypeStruct((8, 2048), F32),
                   jax.ShapeDtypeStruct((8, 1024), F32), jax.ShapeDtypeStruct((8, 100), F32)],
        in_specs=[hbm, hbm, hbm],
        out_specs=[hbm, vmem, vmem, vmem],
        scratch_shapes=[pltpu.VMEM((128, 1024), F32), pltpu.VMEM((4, 8, 8, 128), F32),
                        pltpu.VMEM((100, 1024), BF), pltpu.VMEM((128, 1024), BF), dma((6,)), dma((4,))],
    )(raw_hidden, raw_sums, head_projection.T)
    return hidden_grad.reshape(2, 64, 1024), kv_grad, out_grad, head_grad


def solution(mesh):
    placed = (
        P("member", "band", None),
        P("band", None),
        P(),
        P(),
        P(),
        P(None, "band"),
        P(None, "band"),
        P("band"),
        P(),
        P(None, "band"),
        P("band", None),
    )
    return jax.shard_map(
        shards,
        mesh=mesh,
        in_specs=placed,
        out_specs=(
            P("member", "band", None),
            P(("member", "band"), None),
            P(("member", "band"), None),
            P(("member", "band"), None),
        ),
        check_vma=False,
    )
```

```python
import jax
import jax.numpy as jnp
from jax import lax
from jax.experimental import pallas as pl
from jax.experimental.pallas import tpu as pltpu
from jax.sharding import PartitionSpec as P

MESH = pl.DeviceIdType.MESH
BF = jnp.bfloat16
F32 = jnp.float32
ALPHA = 0.95
SOFTENING = 0.5
MEMBERS = 16
DEVICES = 128
NN = (((1,), (0,)), ((), ()))
NT = (((1,), (1,)), ((), ()))


def mm(a, b, dims=NN):
    return lax.dot_general(a, b, dims, preferred_element_type=F32)


def rem(a, n):
    return lax.rem(a, jnp.int32(n))


def div(a, n):
    return lax.div(a, jnp.int32(n))


def body(
    hid_hbm, q_hbm, kvw_hbm, ow_hbm, head_hbm, init_hbm, truth_hbm, lat_hbm, cw_hbm, src_hbm, halo_hbm,
    hg_hbm, frcv,
    head, init, truth, lat, cw, src, halo,
    ext, q3, kvw, ow, owt, qt, headp, headt, hgt, pick, lrow, kvo, kvh, vto, mask, gt, dsg, um,
    initp, truthp, wts, f3, fg, lloc, l4, ug, dm, ah, ahx, ahs, ahr, ahs2, ahr2, nown, nsend, nrecv, nt, nsnd,
    nrcv, kvp, kvr, fsnd, hg,
    in_sem, out_sem, halo_s, halo_r, hid_s, hid_r, sib_s, sib_r, fc_s, fc_r, lg_s, lg_r,
    ah_s, ah_r, ay_s, ay_r, nh_s, nh_r, na_s, na_r, rs_s, rs_r, fin_s, fin_r, ax_s, ax_r,
):
    mem, band = lax.axis_index("member"), lax.axis_index("band")
    z, ylo = div(mem, 2), rem(mem, 2)
    core = rem(band, 2)
    group = z * 2 + core
    plane = ylo * 8 + div(band, 2)
    x, yhi = div(band, 4), rem(div(band, 2), 2)
    y = yhi * 2 + ylo
    sibling = (mem, band + 1 - 2 * core)
    below, above = (mem, rem(band + 15, 16)), (mem, rem(band + 1, 16))
    pending = []

    def group_peer(j):
        return div(j, 2) * 2 + ylo, band - core + rem(j, 2)

    def plane_peer(q):
        return z * 2 + div(q, 8), rem(q, 8) * 2 + core

    def member_peer(m):
        return m, band

    def remote(source, target, send, recv, device):
        return pltpu.make_async_remote_copy(
            src_ref=source, dst_ref=target, send_sem=send, recv_sem=recv,
            device_id=device, device_id_type=MESH)

    def sent(bulk, send, recv):
        pending.append(remote(bulk, bulk, send, recv, sibling))

    def received(bulk, send, recv):
        remote(bulk, bulk, send, recv, sibling).wait_recv()

    def flush():
        while pending:
            pending.pop(0).wait_send()

    loads = [pltpu.make_async_copy(source, target, in_sem.at[i]) for i, (source, target) in enumerate([
        (halo_hbm, halo), (hid_hbm, ext.at[:, 0:2]), (src_hbm, src), (lat_hbm, lat), (cw_hbm, cw),
        (init_hbm, init), (truth_hbm, truth), (head_hbm, head), (ow_hbm, ow), (kvw_hbm, kvw)])]
    loads += [pltpu.make_async_copy(q_hbm.at[:, 128 * p:128 * p + 128], q3.at[p], in_sem.at[10 + p])
              for p in range(8)]
    loads[0].start()
    loads[1].start()

    barrier = pltpu.get_barrier_semaphore()

    def greet(device):
        pl.semaphore_signal(barrier, inc=1, device_id=device, device_id_type=MESH)

    for k in (10, 9, 11, 6, 5, 7, 8, 2, 13, 14, 3, 1, 15, 4, 12):
        greet(plane_peer(rem(plane + k, 16)))
    greet(below)
    greet(above)
    for k in range(4):
        greet(member_peer(rem(mem + 2 * k + 1, 8)))
    for k in range(1, 8):
        greet(group_peer(rem(group + k, 8)))

    loads[0].wait()
    for m in range(2):
        for d in range(2):
            at = 64 * d + 32 * m
            lrow[0:1, at:at + 32] = halo[d:d + 1, :] + 64 * m
    row_of = lax.broadcasted_iota(jnp.int32, (128, 128), 0)
    lane_of = lax.broadcasted_iota(jnp.int32, (128, 128), 1)
    scatter = (row_of == lrow[0:1, :]).astype(F32)
    gather = scatter.T.astype(BF)
    scatter = scatter.astype(BF)

    loads[1].wait()
    for copy in loads[2:8] + loads[10:] + loads[8:10]:
        copy.start()
    own = ext[:, 0:2].reshape(128, 1024)
    for n in range(4):
        cols = slice(256 * n, 256 * n + 256)
        pick[:, :, :, cols] = mm(gather, own[:, cols]).astype(BF).reshape(2, 2, 32, 256)

    pl.semaphore_wait(barrier, 28)
    to_below = remote(pick.at[0], ext.at[:, 3], halo_s.at[0], halo_r.at[0], below)
    to_above = remote(pick.at[1], ext.at[:, 2], halo_s.at[1], halo_r.at[1], above)
    to_below.start()
    to_above.start()
    pending.extend([to_below, to_above])

    for n in range(8):
        rows = slice(128 * n, 128 * n + 128)
        hgt[group, rows, :] = own[:, rows].T
    pieces = (pl.ds(0, 256), pl.ds(256, 256), pl.ds(512, 512))

    def hid_piece(a, j):
        return hgt.at[j, pieces[a]]

    def hid_bulk(a):
        return hgt.at[0:3, pieces[a]]

    def hid_send(a):
        for k in (2, 1, 3):
            remote(hid_piece(a, group), hid_piece(a, group), hid_s.at[a], hid_r.at[a],
                   group_peer(rem(group + 2 * k, 8))).start()
        sent(hid_bulk(a), hid_s.at[a], hid_r.at[a])

    def hid_forward(a):
        received(hid_bulk(a), hid_s.at[a], hid_r.at[a])
        for k in (1, 2, 3):
            block = hid_piece(a, rem(group + 2 * k, 8))
            remote(block, block, sib_s.at[a], sib_r.at[a], sibling).start()
        sent(hid_bulk(a), sib_s.at[a], sib_r.at[a])

    hid_send(0)
    remote(hgt.at[group], hgt.at[group], sib_s.at[3], sib_r.at[3], sibling).start()
    sent(hgt.at[0], sib_s.at[3], sib_r.at[3])

    for copy in loads[2:8]:
        copy.wait()
    headt[...] = jnp.zeros_like(headt)
    headt[0:100, :] = head[...]
    headp[...] = headt[...].T
    initp[...] = jnp.zeros_like(initp)
    initp[0:100, :] = init[...]
    truthp[...] = jnp.zeros_like(truthp)
    truthp[0:100, :] = truth[...]
    wts[...] = jnp.zeros_like(wts)
    wts[0:1, 0:100] = cw[...]
    diag = jnp.where(row_of == lane_of, wts[0:1, 0:128], 0.0)
    wts[...] = jnp.sum(diag, axis=1, keepdims=True) * lat[...]
    point_row = lax.broadcasted_iota(jnp.int32, (128, 256), 0)
    edge = (point_row == src[0:1, :]) | (point_row == src[1:2, :]) | (point_row == src[2:3, :])
    edge = edge.astype(F32)
    for at in (0, 64):
        mask[at:at + 64, :] = edge[0:64]
        mask[128 + at:128 + at + 64, :] = edge[64:128]
    lo_lane = (lane_of < 64).astype(BF)[0:64]
    hi_lane = (lane_of >= 64).astype(BF)[0:64]
    for p in range(8):
        loads[10 + p].wait()
        qt[128 * p:128 * p + 128, :] = q3[p].T
    loads[8].wait()
    for i in range(4):
        rows = slice(256 * i, 256 * i + 256)
        for j in range(4):
            cols = slice(256 * j, 256 * j + 256)
            owt[rows, cols] = ow[cols, rows].T

    def project(rows, target, parts=range(8)):
        for n in parts:
            part = mm(rows, kvw[:, 256 * n:256 * n + 256]).astype(BF)
            target[2 * n] = part[:, :128]
            target[2 * n + 1] = part[:, 128:]

    def by_head(block):
        return jnp.concatenate([block * lo_lane, block * hi_lane], axis=0)

    def gates(part, source, m, p):
        at = slice(128 * part, 128 * part + 128)
        score = mm(by_head(source[p, 64 * m:64 * m + 64, :]), q3[p], NT)
        th = jnp.tanh(score * (0.5 / 8.0))
        on = mask[at, :]
        gate = ((0.5 + 0.5 * th) * on).astype(BF)
        gt[m, p, at, :] = gate
        dsg[m, p, at, :] = (0.25 - 0.25 * th * th) * (on * 0.125)
        return gate

    loads[9].wait()
    project(own, kvo)
    for m in range(2):
        for p in range(8):
            gates(0, kvo, m, p)
            vto[m, p] = by_head(kvo[8 + p, 64 * m:64 * m + 64, :]).T
    to_below.wait_recv()
    to_above.wait_recv()
    received_rows = ext[:, 2:4].reshape(128, 1024)

    my_rows = pl.ds(pl.multiple_of(mem * 16, 16), 16)
    for m in range(2):
        for p in range(8):
            if m == 0 and p % 2 == 0:
                project(received_rows, kvh, (p // 2, 4 + p // 2))
            gate = jnp.concatenate([gt[m, p, 0:128, :], gates(1, kvh, m, p)], axis=0)
            value = by_head(kvh[8 + p, 64 * m:64 * m + 64, :]).T
            value = jnp.concatenate([vto[m, p], value], axis=1)
            um[m, 128 * p:128 * p + 128, :] = mm(value, gate).astype(BF)
        merged = um[m, 0:1024, :]
        for i in range(4):
            rows = slice(256 * i, 256 * i + 256)
            up = mm(owt[rows, :], merged) + qt[rows, :].astype(F32)
            um[m, 1024 + 256 * i:1024 + 256 * i + 256, :] = up.astype(BF)
        f3[m] = mm(headt[...], um[m, 1024:2048, :]) + initp[...]
        for k in range(7, 0, -1):
            to = rem(mem + k, 8)
            remote(f3.at[m, pl.ds(pl.multiple_of(to * 16, 16), 16), :], fg.at[2 * mem + m],
                   fc_s.at[m], fc_r.at[m], member_peer(to)).start()
        sent(fg.at[0:7], fc_s.at[m], fc_r.at[m])
        fg[2 * mem + m] = f3[m, my_rows, :]

    hid_forward(0)
    hid_send(1)
    for m in range(2):
        received(fg.at[0:7], fc_s.at[m], fc_r.at[m])

    spread = (1.0 - (1.0 - ALPHA) / MEMBERS) / (MEMBERS * (MEMBERS - 1))
    soft = SOFTENING * SOFTENING
    truth_rows = truthp[my_rows, :]
    weight = wts[my_rows, :]

    def loss(k):
        to = rem(mem + k, 8)
        for i in range(2):
            f = fg[2 * to + i]
            gap = f[None] - fg[...]
            slopes = jnp.sum(gap * lax.rsqrt(gap * gap + soft), axis=0)
            off = f - truth_rows
            slope = off * lax.rsqrt(off * off + soft)
            lloc[2 * to + i] = (weight * (slope * (1.0 / MEMBERS) - spread * slopes)).astype(BF)

    for part in ((4, 3, 5), (2, 6, 1), (7, 0)):
        for k in part:
            loss(k)
        for k in part:
            if k:
                to = rem(mem + k, 8)
                remote(lloc.at[pl.ds(2 * to, 2)], l4.at[:, mem], lg_s, lg_r, member_peer(to)).start()
    sent(lloc.at[0:14], lg_s, lg_r)
    hid_forward(1)
    for m in range(2):
        l4[m, mem] = lloc[2 * mem + m]
    received(lloc.at[0:14], lg_s, lg_r)
    hid_send(2)

    for m in range(2):
        grad = l4[m].reshape(128, 256)
        for i in range(4):
            rows = slice(256 * i, 256 * i + 256)
            ug[m, rows, :] = mm(headp[rows, :], grad).astype(BF)
    low = (lane_of < 64)[0:64]
    order = (2, 1, 3, 0)

    def back_copy(h, step, d, inward=False):
        side = d if inward else 1 - d
        return remote(nsend.at[d, h, step], nrecv.at[h, step, side], nh_s.at[h, step, d],
                      nh_r.at[h, step, side], (below, above)[d])

    def keep(h, step, i, m, both):
        cols = slice(128 * i, 128 * i + 128)
        nown[h, step, 64 * m:64 * m + 64, cols] = jnp.where(low, both[0:64], both[64:128])
        halo_part = jnp.where(low, both[128:192], both[192:256]).astype(BF)
        nsend[0, h, step, m, :, cols] = halo_part[0:32]
        nsend[1, h, step, m, :, cols] = halo_part[32:64]

    def send_back(h, step):
        for d in range(2):
            copy = back_copy(h, step, d)
            copy.start()
            pending.append(copy)

    def merged_grad(step):
        rows = pl.ds(pl.multiple_of(rem(z + order[step], 4) * 256, 256), 256)
        for m in range(2):
            dm[step, m] = mm(ow[rows, :], ug[m]).astype(BF)

    merged_grad(0)
    for step in range(4):
        for i in range(2):
            for m in range(2):
                p = 2 * rem(z + order[step], 4) + i
                keep(0, step, i, m, mm(gt[m, p], dm[step, m, 128 * i:128 * i + 128, :], NT))
        if step < 3:
            merged_grad(step + 1)
        send_back(0, step)

    def score_grads(step):
        grads = []
        for i in range(2):
            for m in range(2):
                p = 2 * rem(z + order[step], 4) + i
                value = jnp.concatenate([by_head(kvo[8 + p, 64 * m:64 * m + 64, :]),
                                         by_head(kvh[8 + p, 64 * m:64 * m + 64, :])], axis=0)
                gate_grad = mm(value, dm[step, m, 128 * i:128 * i + 128, :])
                grads.append((gate_grad * dsg[m, p]).astype(BF))
        return grads

    ready = score_grads(0)

    for a in range(2):
        for i in range(4):
            rows = slice(1024 * a + 256 * i, 1024 * a + 256 * i + 256)
            both = mm(um[0, rows, :], l4[0].reshape(128, 256), NT) + mm(
                um[1, rows, :], l4[1].reshape(128, 256), NT)
            ah[i % 2, a, i // 2] = both.astype(BF)
    swap = remote(ah.at[1 - core], ahx, ax_s, ax_r, sibling)
    swap.start()
    pending.append(swap)

    for step in range(4):
        for i in range(2):
            for m in range(2):
                p = 2 * rem(z + order[step], 4) + i
                keep(1, step, i, m, mm(ready[2 * i + m], q3[p]))
        if step < 3:
            ready = score_grads(step + 1)
        send_back(1, step)

    def node_step(h, step):
        g = rem(z + order[step], 4)
        for d in range(2):
            back_copy(h, step, d, True).wait_recv()
        total = (nown[h, step] + mm(scatter, nrecv[h, step].reshape(128, 256))).astype(BF)
        for c in range(2):
            nsnd[h, step, c] = total[:, 128 * c:128 * c + 128]
        if step < 3:
            for c in range(2):
                remote(nsnd.at[h, step, c], nrcv.at[h, group], na_s.at[h], na_r.at[h],
                       group_peer(2 * g + c)).start()
        else:
            remote(nsnd.at[h, 3, 1 - core], nrcv.at[h, group], na_s.at[h], na_r.at[h], sibling).start()
            sent(nrcv.at[h, 0:7], na_s.at[h], na_r.at[h])
            nrcv[h, group] = nsnd[h, 3, core]
        nt[:, pl.ds(pl.multiple_of(1024 * (1 - h) + g * 256, 256), 256)] = total

    swap.wait_recv()
    for a in range(2):
        for i in range(2):
            both = ah[core, a, i].astype(F32) + ahx[a, i].astype(F32)
            both = both.astype(BF).reshape(2, 4, 2, 16, 128)
            for to in range(4):
                ahs[to, a, i] = both[:, to]
    for k in (2, 1, 3):
        to = rem(x + k, 4)
        remote(ahs.at[to], ahr.at[x], ah_s, ah_r, (mem, band + 4 * (to - x))).start()
    sent(ahr.at[0:3], ah_s, ah_r)
    ahr[x] = ahs[x]

    for step in range(4):
        node_step(0, step)
    hid_forward(2)


    for step in range(4):
        node_step(1, step)

    received(hgt.at[0], sib_s.at[3], sib_r.at[3])
    for a in range(3):
        received(hid_bulk(a), sib_s.at[a], sib_r.at[a])
    for h in range(2):
        received(nrcv.at[h, 0:7], na_s.at[h], na_r.at[h])
        node_cols = nrcv[h].reshape(1024, 128)
        for i in range(4):
            rows = slice(256 * i, 256 * i + 256)
            left = jnp.concatenate([hgt[j, rows, :] for j in range(8)], axis=1)
            kvp[h, :, i] = mm(left, node_cols).astype(BF).reshape(16, 16, 128)
        for k in range(1, 16):
            to = rem(plane + k, 16)
            remote(kvp.at[h, to], kvr.at[h, plane], rs_s.at[h], rs_r.at[h], plane_peer(to)).start()
        kvr[h, plane] = kvp[h, plane]
        if h:
            continue
        received(ahr.at[0:3], ah_s, ah_r)
        both = jnp.sum(ahr[...].astype(F32), axis=0).astype(BF)
        for to in range(4):
            ahs2[to] = both[:, :, to % 2, to // 2]
        for k in range(1, 4):
            to = rem(y + k, 4)
            remote(ahs2.at[to], ahr2.at[y], ay_s, ay_r,
                   (z * 2 + rem(to, 2), x * 4 + div(to, 2) * 2 + core)).start()
        sent(ahr2.at[0:3], ay_s, ay_r)
        ahr2[y] = ahs2[y]

    for i in range(4):
        rows = slice(256 * i, 256 * i + 256)
        hg[:, rows] = mm(nt[...], kvw[rows, :], NT)
    hg_copy = pltpu.make_async_copy(hg, hg_hbm, out_sem)
    hg_copy.start()
    flush()

    def fin_send(part, sem):
        for k in (4, 5, 2, 3, 6, 7, 1):
            to = rem(group + k, 8)
            remote(fsnd.at[part, to], frcv.at[part, group], fin_s.at[sem], fin_r.at[sem],
                   group_peer(to)).start()
        bulk = frcv.at[part, 0:7]
        sent(bulk, fin_s.at[sem], fin_r.at[sem])

    received(ahr2.at[0:3], ay_s, ay_r)
    ah_sum = jnp.sum(ahr2[...].astype(F32), axis=0)
    for i in range(2):
        for c in range(2):
            at = (2 * i + core) * 2 + c
            other = (2 * i + 1 - core) * 2 + c
            for a in range(2):
                fsnd[2 + a, at] = ah_sum[a, i, 8 * c:8 * c + 8]
                fsnd[2 + a, other] = jnp.zeros((8, 128), F32)
    for part in (2, 3):
        fin_send(part, part)
        frcv[part, group] = fsnd[part, group]
    for h in range(2):
        received(kvr.at[h, 0:15], rs_s.at[h], rs_r.at[h])
        fsnd[h] = jnp.sum(kvr[h].astype(F32), axis=0).reshape(8, 8, 128)
        fin_send(h, h)
        frcv[h, group] = fsnd[h, group]
    for h in range(2):
        sent(kvr.at[h, 0:15], rs_s.at[h], rs_r.at[h])
    flush()
    hg_copy.wait()
    for part in (2, 3, 0, 1):
        received(frcv.at[part, 0:7], fin_s.at[part], fin_r.at[part])


def finish(hg_hbm, frcv_hbm, head_hbm, hg_out, kv_out, og_out, hd_out, hg, frcv, head, headt, sem, out_sem):
    loads = [pltpu.make_async_copy(frcv_hbm, frcv, sem.at[4]),
             pltpu.make_async_copy(head_hbm, head, sem.at[5])]
    quarters = [pl.ds(32 * i, 32) for i in range(4)]
    loads += [pltpu.make_async_copy(hg_hbm.at[q], hg.at[q], sem.at[i]) for i, q in enumerate(quarters)]
    for copy in loads:
        copy.start()
    stores = [pltpu.make_async_copy(hg.at[q], hg_out.at[q], out_sem.at[i]) for i, q in enumerate(quarters)]
    headt[...] = jnp.zeros_like(headt)
    for load, store in zip(loads[2:], stores):
        load.wait()
        store.start()
    loads[0].wait()
    loads[1].wait()
    headt[0:100, :] = head[...]
    for j in range(8):
        at = 128 * j
        kv_out[:, at:at + 128] = frcv[1, j] * (1.0 / DEVICES)
        kv_out[:, 1024 + at:1024 + at + 128] = frcv[0, j] * (1.0 / DEVICES)
    sums = jnp.sum(frcv[2:4], axis=1) * (1.0 / DEVICES)
    hd_out[...] = sums[1, :, 0:100]
    outer = sums[0]
    big = outer.astype(BF)
    small = (outer - big.astype(F32)).astype(BF)
    og_out[...] = mm(big, headt[...]) + mm(small, headt[...])
    for copy in stores:
        copy.wait()


def shards(hidden, queries, kv_weight, out_weight, head_projection, initial_state, truth,
           latitude_weight, channel_loss_weight, sources, halo_rows):
    vmem = pl.BlockSpec(memory_space=pltpu.VMEM)
    hbm = pl.BlockSpec(memory_space=pl.ANY)
    dma = pltpu.SemaphoreType.DMA
    scratch = [
        ((100, 1024), BF), ((100, 256), F32), ((100, 256), F32), ((1, 256), F32), ((1, 100), F32),
        ((3, 256), jnp.int32), ((2, 32), jnp.int32),
        ((2, 4, 32, 1024), BF), ((8, 256, 128), BF), ((1024, 2048), BF), ((1024, 1024), BF),
        ((1024, 1024), BF), ((1024, 256), BF), ((1024, 128), BF), ((128, 1024), BF),
        ((8, 1024, 128), BF), ((2, 2, 32, 1024), BF), ((8, 128), jnp.int32), ((16, 128, 128), BF),
        ((16, 128, 128), BF), ((2, 8, 128, 128), BF),
        ((256, 256), F32), ((2, 8, 256, 256), BF), ((2, 8, 256, 256), F32), ((2, 2048, 256), BF),
        ((128, 256), F32), ((128, 256), F32), ((128, 256), F32), ((2, 128, 256), F32),
        ((16, 16, 256), F32), ((16, 16, 256), BF), ((2, 8, 16, 256), BF), ((2, 1024, 256), BF),
        ((4, 2, 256, 256), BF), ((2, 2, 2, 256, 128), BF), ((2, 2, 256, 128), BF),
        ((4, 2, 2, 2, 2, 16, 128), BF), ((4, 2, 2, 2, 2, 16, 128), BF),
        ((4, 2, 2, 16, 128), BF), ((4, 2, 2, 16, 128), BF),
        ((2, 4, 128, 256), F32), ((2, 2, 4, 2, 32, 256), BF), ((2, 4, 2, 2, 32, 256), BF),
        ((128, 2048), BF), ((2, 4, 2, 128, 128), BF), ((2, 8, 128, 128), BF),
        ((2, 16, 4, 16, 128), BF), ((2, 16, 4, 16, 128), BF), ((4, 8, 8, 128), F32),
        ((128, 1024), F32),
    ]
    sems = [(18,), (), (2,), (2,), (3,), (3,), (4,), (4,), (2,), (2,), (), (), (), (), (), (), (2, 4, 2),
            (2, 4, 2), (2,), (2,), (2,), (2,), (4,), (4,), (), ()]
    raw_hidden, raw_sums = pl.pallas_call(
        body,
        out_shape=[jax.ShapeDtypeStruct((128, 1024), F32), jax.ShapeDtypeStruct((4, 8, 8, 128), F32)],
        in_specs=[hbm] * 11,
        out_specs=[hbm, vmem],
        scratch_shapes=[pltpu.VMEM(shape, kind) for shape, kind in scratch] + [dma(n) for n in sems],
        compiler_params=pltpu.CompilerParams(
            collective_id=0, has_side_effects=True, vmem_limit_bytes=56 * 1024 * 1024),
    )(
        hidden.reshape(2, 2, 32, 1024), queries, kv_weight, out_weight, head_projection.T,
        initial_state, truth, latitude_weight.reshape(1, 256), channel_loss_weight.reshape(1, 100),
        sources, halo_rows,
    )
    hidden_grad, kv_grad, out_grad, head_grad = pl.pallas_call(
        finish,
        out_shape=[jax.ShapeDtypeStruct((128, 1024), F32), jax.ShapeDtypeStruct((8, 2048), F32),
                   jax.ShapeDtypeStruct((8, 1024), F32), jax.ShapeDtypeStruct((8, 100), F32)],
        in_specs=[hbm, hbm, hbm],
        out_specs=[hbm, vmem, vmem, vmem],
        scratch_shapes=[pltpu.VMEM((128, 1024), F32), pltpu.VMEM((4, 8, 8, 128), F32),
                        pltpu.VMEM((100, 1024), BF), pltpu.VMEM((128, 1024), BF), dma((6,)), dma((4,))],
    )(raw_hidden, raw_sums, head_projection.T)
    return hidden_grad.reshape(2, 64, 1024), kv_grad, out_grad, head_grad


def solution(mesh):
    placed = (
        P("member", "band", None),
        P("band", None),
        P(),
        P(),
        P(),
        P(None, "band"),
        P(None, "band"),
        P("band"),
        P(),
        P(None, "band"),
        P("band", None),
    )
    return jax.shard_map(
        shards,
        mesh=mesh,
        in_specs=placed,
        out_specs=(
            P("member", "band", None),
            P(("member", "band"), None),
            P(("member", "band"), None),
            P(("member", "band"), None),
        ),
        check_vma=False,
    )
```
